128 devices in a mesh: seq: 16 (over x, z_hi, core), tp: 8 (over z_lo, y).
Axes of the slice: x: 4, y: 4, z: 4 (z_hi: 2, z_lo: 2; z = z_hi * 2 + z_lo), core: 2. Of those that a mesh axis runs over, the one named last changes fastest.
Arguments:
- queries: bfloat16 [8192, 64, 128], P('seq', 'tp'), may hold values from -8 to 8
- key_heads: bfloat16 [8192, 8, 128], P('seq', 'tp'), may hold values from -8 to 8
- value_heads: bfloat16 [8192, 8, 128], P('seq', 'tp'), may hold values from -16 to 16
- out_weight: bfloat16 [8192, 5120], P('tp'), may hold values from -0.0625 to 0.0625
- doc_lengths: int32 [4], replicated, may hold values from 1 to 4096, 8192 in all
- piece_owner: int32 [256], replicated, may hold values from 0 to 15, as said below
Outputs:
- mixed: bfloat16 [8192, 5120], P('seq', 'tp')
The draws below stay inside these ranges and needn't reach their ends.
Inputs may be any that keep to these rules, and one draw needn't show every extreme that they name: Piece p of piece_owner covers tokens p * 32 to (p + 1) * 32 - 1. Every owner receives exactly 16 pieces, and at most 2 pieces come from the 16 pieces of one device to one owner. `doc_lengths`: the documents fill all 8192 tokens; the longest holds half of 8192.
All inputs are finite; a program needn't handle non-finite values.
Results may differ from the reference program's by a relative error of at most 0.019.
Values may be sent and summed in bfloat16 or wider, within the bound.
A program may use at most 64 MiB of HBM per device.

```python
import math
import jax
import jax.numpy as jnp
import numpy as np
from jax import lax

D = 5120
HEADS = 64
KV_HEADS = 8
HD = 128
NDOCS = 4
PIECES = 16
TOKENS = 8192
PIECE = 32
NPIECES = 256


def draw_queries(key, part):
    key = jax.random.fold_in(key, 7)
    first_key = jax.random.fold_in(key, 0)
    full_shape = (TOKENS, HEADS, HD)
    result = jnp.clip(jax.random.normal(first_key, full_shape, jnp.float32), -8.0, 8.0)
    return result.astype(jnp.bfloat16)


def draw_key_heads(key, part):
    key = jax.random.fold_in(key, 13)
    first_key = jax.random.fold_in(key, 0)
    full_shape = (TOKENS, KV_HEADS, HD)
    result = jnp.clip(jax.random.normal(first_key, full_shape, jnp.float32), -8.0, 8.0)
    return result.astype(jnp.bfloat16)


def draw_piece_owner(key, part):
    key = jax.random.fold_in(key, 29)
    first_key, second_key, third_key = jax.random.split(key, 3)
    seq_count = NPIECES // PIECES
    relabel = jax.random.permutation(first_key, seq_count)
    offsets = jax.random.permutation(second_key, seq_count)[:PIECES - 1]
    doubled = jnp.concatenate([offsets[:1], offsets])
    shuffled = jax.random.permutation(third_key, PIECES)
    chosen = doubled[shuffled]
    source_ids = jnp.arange(seq_count)[:, None]
    owners = relabel[(source_ids + chosen[None, :]) % seq_count]
    return owners.reshape(NPIECES).astype(jnp.int32)


def block_levels(rng, dims, cuts, smallest, top_value):
    def one(position, shards_of):
        draws = jax.random.uniform(jax.random.fold_in(jax.random.fold_in(rng, 6), position), (shards_of,), jnp.float32, smallest / len(cuts), top_value / len(cuts))
        return jnp.repeat(jnp.exp(draws), dims[position] // shards_of).reshape((-1,) + (1,) * (len(dims) - position - 1))

    level = one(*cuts[0])
    for cut in cuts[1:]:
        level = level * one(*cut)
    return level


def split_up(amount, total, reach, lean):
    loads = [(1 << 20) // math.isqrt(grade ** lean) + 1 for grade in range(2, amount + 1)]
    spare, holding = total - reach - (amount - 1), [1] * (amount - 1)
    while spare > 0:
        candidates = [i for i in range(amount - 1) if holding[i] < reach]
        whole, budget = sum([loads[i] for i in candidates]), spare
        for i in candidates:
            more = min(reach - holding[i], max(1, budget * loads[i] // whole), spare)
            holding[i] = holding[i] + more
            spare = spare - more
    return np.array([reach] + holding)


def ragged_sizes(rng, count, total, bound, slope):
    if count == 2:
        one = jax.random.randint(rng, (), max(1, total - bound), min(bound, total - 1) + 1)
        return jnp.stack([one, total - one])
    lengths = jnp.asarray(split_up(count, total, bound, slope), jnp.int32)
    pairs = (count - 1) // 2
    donor, receiver = lengths[1:1 + 2 * pairs:2], lengths[2:2 + 2 * pairs:2]
    room = jnp.minimum(donor - 1, bound - receiver)
    shifted = jax.random.randint(jax.random.fold_in(rng, 1), (pairs,), 0, 1 << 20) % (room + 1)
    lengths = lengths.at[1:1 + 2 * pairs:2].set(donor - shifted).at[2:2 + 2 * pairs:2].set(receiver + shifted)
    return lengths[jax.random.permutation(jax.random.fold_in(rng, 2), count)]


def bell_draw(own_key, extent, scale, reach, cuts=(), kind=jnp.bfloat16):
    values = jax.random.normal(own_key, extent, jnp.float32) * scale
    if len(cuts) > 0:
        values = block_levels(own_key, extent, cuts, -0.22, 0.18) * values
    return jnp.clip(values, min=-reach, max=reach).astype(kind)


def setup_inputs(seed: int = 0) -> dict:
    keys = jax.random.split(jax.random.key(seed), 7)
    queries = draw_queries(jax.random.fold_in(keys[6], 71), 0)
    key_heads = draw_key_heads(jax.random.fold_in(keys[6], 71), 0)
    value_heads = bell_draw(keys[2], (TOKENS, KV_HEADS, HD), 4.0, 16.0, ((0, 16), (1, 8)))
    out_weight = bell_draw(keys[3], (HEADS * HD, D), (HEADS * HD) ** -0.5, 0.0625, ((0, 8),))
    doc_lengths = ragged_sizes(keys[4], NDOCS, TOKENS, TOKENS // 2, 2).astype(jnp.int32)
    piece_owner = draw_piece_owner(jax.random.fold_in(keys[6], 71), 0)
    return dict(queries=queries, key_heads=key_heads, value_heads=value_heads, out_weight=out_weight, doc_lengths=doc_lengths, piece_owner=piece_owner)


MASKED = -1e30


def doc_starts(doc_lengths, positions):
    doc_ends = jnp.cumsum(doc_lengths).astype(jnp.int32)
    ended = doc_ends[None, :] <= positions[:, None]
    return jnp.sum(jnp.where(ended, doc_lengths[None, :], 0), axis=1).astype(jnp.int32)


def reference(queries, key_heads, value_heads, out_weight, doc_lengths, piece_owner):
    per_group = HEADS // KV_HEADS
    block_rows = math.gcd(TOKENS, 512)
    block_count = TOKENS // block_rows
    window = min(TOKENS, TOKENS // 2 + block_rows)
    starts = doc_starts(doc_lengths, jnp.arange(TOKENS, dtype=jnp.int32))
    score_scale = HD ** -0.5

    def one_block(tile_index):
        group_id = tile_index // block_count
        row_first = (tile_index % block_count) * block_rows
        key_first = jnp.maximum(row_first + block_rows - window, 0).astype(jnp.int32)
        zero_index = jnp.int32(0)
        query_tile = lax.dynamic_slice(queries, (row_first, group_id * per_group, zero_index), (block_rows, per_group, HD)).astype(jnp.float32)
        key_tile = lax.dynamic_slice(key_heads, (key_first, group_id, zero_index), (window, 1, HD))[:, 0].astype(jnp.float32)
        value_tile = lax.dynamic_slice(value_heads, (key_first, group_id, zero_index), (window, 1, HD))[:, 0].astype(jnp.float32)
        query_pos = row_first + jnp.arange(block_rows, dtype=jnp.int32)
        key_pos = key_first + jnp.arange(window, dtype=jnp.int32)
        query_start = lax.dynamic_slice(starts, (row_first,), (block_rows,))
        visible = (key_pos[None, :] >= query_start[:, None]) & (key_pos[None, :] <= query_pos[:, None])
        scores = jnp.einsum("qgd,kd->gqk", query_tile, key_tile, precision=lax.Precision.HIGHEST) * score_scale
        scores = jnp.where(visible[None], scores, MASKED)
        row_max = jnp.max(scores, axis=-1, keepdims=True)
        weights = jnp.where(visible[None], jnp.exp(scores - row_max), 0.0)
        run_sum = jnp.sum(weights, axis=-1)
        weights_low = lax.optimization_barrier(weights.astype(jnp.bfloat16)).astype(jnp.float32)
        attended = jnp.einsum("gqk,kd->gqd", weights_low, value_tile, precision=lax.Precision.HIGHEST) / run_sum[..., None]
        return attended.astype(jnp.bfloat16)

    tile_stack = lax.map(one_block, jnp.arange(KV_HEADS * block_count, dtype=jnp.int32))
    attended = tile_stack.reshape(KV_HEADS, block_count, per_group, block_rows, HD)
    attended = jnp.transpose(attended, (1, 3, 0, 2, 4)).reshape(TOKENS, HEADS * HD)
    projected = jnp.dot(attended, out_weight, preferred_element_type=jnp.float32).astype(jnp.bfloat16)
    piece_order = jnp.argsort(piece_owner, stable=True)
    return projected.reshape(NPIECES, PIECE, D)[piece_order].reshape(TOKENS, D)
```

```python
import functools

import jax
import jax.numpy as jnp
from jax import lax
from jax.experimental import pallas as pl
from jax.experimental.pallas import tpu as pltpu
from jax.sharding import PartitionSpec as P

MASKED = -1e30
BF16, F32, I32 = jnp.bfloat16, jnp.float32, jnp.int32
ROWS = 512
HEADS = 8
HD = 128
HALF = 256
GROUP = 3
SPAN = GROUP * ROWS
BACK = 8
SCORE = HD**-0.5 * 1.4426950408889634
MESH = pl.DeviceIdType.MESH


def places():
    s = lax.axis_index("seq")
    x, z, core = s // 4, (s // 2) % 2, s % 2

    def at(step, flip_z, flip_core):
        return ((x + step) % 4) * 4 + ((z + flip_z) % 2) * 2 + (core + flip_core) % 2

    return s, z, core, at


def slot(ref_k, ref_v, delta):
    g, r = delta // GROUP, delta % GROUP
    start = pl.multiple_of(r * ROWS, ROWS)
    return (
        ref_k.at[g, pl.ds(start, ROWS), pl.ds(0, HD)],
        ref_v.at[g, pl.ds(0, HD), pl.ds(start, ROWS)],
    )


def doc_of(ends, positions):
    doc = jnp.where(positions < 0, -1, 0)
    for end in ends:
        doc = doc + jnp.where(positions >= end, 1, 0)
    return doc


def attend_kernel(
    q_ref, k_ref, v_ref, len_ref, o_ref, qx, kx, vx, acc, top, diff, s0, s1, p0, p1, send, recv
):
    s, z, core, at = places()
    sibling, next_x, prev_x, far_x, other_z = (
        at(0, 0, 1),
        at(1, 0, 0),
        at(3, 0, 0),
        at(2, 0, 0),
        at(0, 1, 0),
    )
    barrier = pltpu.get_barrier_semaphore()
    for peer in (sibling, next_x, prev_x, far_x, other_z):
        pl.semaphore_signal(barrier, inc=1, device_id={"seq": peer}, device_id_type=MESH)

    kx[0, :ROWS, :HD] = k_ref[...]
    vx[0, :HD, :ROWS] = v_ref[...].T
    pl.semaphore_wait(barrier, 5)

    sends = []

    def copies(index, source, target, peer):
        for part, (a, b) in enumerate(zip(slot(kx, vx, source), slot(kx, vx, target))):
            yield pltpu.make_async_remote_copy(
                src_ref=a,
                dst_ref=b,
                send_sem=send.at[index, part],
                recv_sem=recv.at[target, part],
                device_id={"seq": peer},
                device_id_type=MESH,
            )

    def go(index, source, target, peer):
        for copy in copies(index, source, target, peer):
            copy.start()

    def arrived(target):
        for copy in copies(0, 0, target, sibling):
            copy.wait_recv()

    def to_sibling(i):
        go(4 + i, 2 * i + 2 * core, 2 * i + 1, sibling)

    def to_z(i):
        go(2 + i, 4 * z + 4 * i, 2 + 4 * i, other_z)

    go(0, 0, 4, next_x)

    @pl.when(z == 0)
    def _():
        to_z(0)

    @pl.when(core == 0)
    def _():
        to_sibling(0)

    go(1, 0, 8, far_x)

    ends = []
    total = 0
    for d in range(4):
        total = total + len_ref[d]
        ends.append(total)
    lane = lax.broadcasted_iota(I32, (ROWS, HD), 1)
    row = lax.broadcasted_iota(I32, (ROWS, HD), 0)
    mine = jnp.where(doc_of(ends, row + s * ROWS) == lane, MASKED, 0.0).astype(BF16)
    for h in range(HEADS):
        for half in range(2):
            rows = pl.ds(half * HALF, HALF)
            qx[half, h, :, :HD] = q_ref[rows, pl.ds(h * HD, HD)]
            qx[half, h, :, HD:] = mine[half * HALF : (half + 1) * HALF]

    def mark(delta, _):
        start = pl.multiple_of((delta % GROUP) * ROWS, ROWS)
        seen = doc_of(ends, row + (s - delta) * ROWS) == lane
        kx[delta // GROUP, pl.ds(start, ROWS), HD:] = jnp.where(seen, 0.0, 1.0).astype(BF16)
        return 0

    lax.fori_loop(0, BACK + 1, mark, 0)
    for g in range(GROUP):
        vx[g, HD:, :] = jnp.ones((16, SPAN), BF16)
    diff[...] = lax.broadcasted_iota(I32, (ROWS, HALF), 0) - lax.broadcasted_iota(
        I32, (ROWS, HALF), 1
    )
    acc[...] = jnp.zeros_like(acc)
    top[...] = jnp.full_like(top, MASKED)

    arrived(4)

    @pl.when(z == 1)
    def _():
        to_z(0)

    @pl.when(z == 0)
    def _():
        to_z(1)

    @pl.when(core == 0)
    def _():
        to_sibling(2)

    @pl.when(core == 1)
    def _():
        to_sibling(1)

    arrived(2)

    @pl.when(core == 0)
    def _():
        to_sibling(1)

    @pl.when(core == 1)
    def _():
        to_sibling(0)

    arrived(1)

    scores, weights = (s0, s1), (p0, p1)

    def matrix(a, b):
        return lax.dot_general(a, b, (((1,), (1,)), ((), ())), preferred_element_type=F32)

    def one_pass(step, _):
        @pl.when(step == 1)
        def _():
            arrived(8)

            @pl.when(z == 1)
            def _():
                to_z(1)

            @pl.when(core == 1)
            def _():
                to_sibling(3)

        @pl.when(step == 2)
        def _():
            arrived(6)

            @pl.when(core == 0)
            def _():
                to_sibling(3)

            @pl.when(core == 1)
            def _():
                to_sibling(2)

            arrived(3)
            arrived(5)

        @pl.when(step == 3)
        def _():
            arrived(7)

        g = jnp.where(step < 2, 0, 1 + step % 2)
        half = jnp.where(step < 2, step, (step - 2) // 2)
        limit = half * HALF + g * SPAN
        factor = {}
        for i in range(HEADS + 2):
            if i < HEADS:
                out = scores[i % 2]
                qh = qx[half, i]
                out[:ROWS] = jnp.where(
                    diff[...] <= limit, matrix(kx[g, :ROWS, :], qh), MASKED
                )
                out[ROWS:] = matrix(kx[g, ROWS:, :], qh)
            if 0 <= i - 1 < HEADS:
                h = i - 1
                sc = scores[h % 2][...]
                before = top[half, h, :1, :]
                now = jnp.maximum(before, jnp.max(sc, axis=0, keepdims=True))
                weights[h % 2][...] = jnp.exp2((sc - now) * SCORE).astype(BF16)
                factor[h] = jnp.exp2((before - now) * SCORE)
                top[half, h, :1, :] = now
            if 0 <= i - 2 < HEADS:
                h = i - 2
                acc[half, h] = acc[half, h] * factor[h] + jnp.dot(
                    vx[g], weights[h % 2][...], preferred_element_type=F32
                )
        return 0

    lax.fori_loop(0, 6, one_pass, 0)

    for half in range(2):
        for h in range(HEADS):
            value = acc[half, h, :HD, :] / acc[half, h, HD : HD + 1, :]
            o_ref[pl.ds(half * HALF, HALF), pl.ds(h * HD, HD)] = value.T.astype(BF16)

    for index in range(4):
        for copy in copies(index, 0, 1, sibling):
            copy.wait_send()
    for i in range(4):
        for copy in copies(4 + i, 0, 1, sibling):
            copy.wait_send()


def attention(queries, key_rows, value_rows, doc_lengths):
    vmem = pl.BlockSpec(memory_space=pltpu.VMEM)
    return pl.pallas_call(
        attend_kernel,
        out_shape=jax.ShapeDtypeStruct((ROWS, HEADS * HD), BF16),
        in_specs=[vmem, vmem, vmem, pl.BlockSpec(memory_space=pltpu.SMEM)],
        out_specs=vmem,
        scratch_shapes=[
            pltpu.VMEM((2, HEADS, HALF, 2 * HD), BF16),
            pltpu.VMEM((GROUP, SPAN, 2 * HD), BF16),
            pltpu.VMEM((GROUP, HD + 16, SPAN), BF16),
            pltpu.VMEM((2, HEADS, HD + 16, HALF), F32),
            pltpu.VMEM((2, HEADS, 8, HALF), F32),
            pltpu.VMEM((ROWS, HALF), I32),
            pltpu.VMEM((SPAN, HALF), F32),
            pltpu.VMEM((SPAN, HALF), F32),
            pltpu.VMEM((SPAN, HALF), BF16),
            pltpu.VMEM((SPAN, HALF), BF16),
            pltpu.SemaphoreType.DMA((8, 2)),
            pltpu.SemaphoreType.DMA((BACK + 1, 2)),
        ],
        compiler_params=pltpu.CompilerParams(
            collective_id=0, has_side_effects=True, vmem_limit_bytes=48 << 20
        ),
    )(queries, key_rows, value_rows, doc_lengths)


def outgoing(piece_owner, device, pieces, seq_count):
    local_owner = lax.dynamic_slice_in_dim(piece_owner, device * pieces, pieces)
    local_order = jnp.arange(pieces, dtype=jnp.int32)
    earlier = (local_owner[None, :] == local_owner[:, None]) & (
        local_order[None, :] < local_order[:, None]
    )
    slot_rank = jnp.sum(earlier.astype(jnp.int32), axis=1)
    target_slot = jnp.arange(seq_count * 2, dtype=jnp.int32)
    select = local_owner[None, :] * 2 + slot_rank[None, :] == target_slot[:, None]
    return select.astype(jnp.bfloat16)


def incoming(piece_owner, device, pieces):
    piece_total = piece_owner.shape[0]
    piece_ids = jnp.arange(piece_total, dtype=jnp.int32)
    is_mine = piece_owner == device
    mine_rank = jnp.cumsum(is_mine.astype(jnp.int32)) - 1
    my_slots = jnp.arange(pieces, dtype=jnp.int32)
    chosen = is_mine[None, :] & (mine_rank[None, :] == my_slots[:, None])
    held_pieces = jnp.sum(jnp.where(chosen, piece_ids[None, :], 0), axis=1)
    source_dev = held_pieces // pieces
    earlier_mine = (
        is_mine[None, :]
        & (piece_ids[None, :] // pieces == source_dev[:, None])
        & (piece_ids[None, :] < held_pieces[:, None])
    )
    slot_rank = jnp.sum(earlier_mine.astype(jnp.int32), axis=1)
    return source_dev * 2 + slot_rank


def route(row_data, select, arrival_slot):
    pieces = select.shape[1]
    row_width = row_data.shape[1]
    piece_len = row_data.shape[0] // pieces
    stacked = row_data.reshape(pieces, piece_len * row_width)
    rows = jnp.dot(select, stacked, preferred_element_type=F32).astype(row_data.dtype)
    rows = rows.reshape(select.shape[0] * piece_len, row_width)
    arrived = lax.all_to_all(rows, "seq", split_axis=0, concat_axis=0, tiled=True)
    arrived = arrived.reshape(select.shape[0], piece_len, row_width)
    return jnp.take(arrived, arrival_slot, axis=0).reshape(pieces * piece_len, row_width)


def on_device(queries, key_heads, value_heads, out_weight, doc_lengths, piece_owner):
    device = lax.axis_index("seq")
    attended = attention(
        queries.reshape(ROWS, HEADS * HD),
        key_heads.reshape(ROWS, HD),
        value_heads.reshape(ROWS, HD),
        doc_lengths,
    )
    partial_sum = jnp.dot(attended, out_weight, preferred_element_type=F32)
    summed = lax.psum_scatter(
        partial_sum.astype(BF16), "tp", scatter_dimension=1, tiled=True
    )
    select = outgoing(piece_owner, device, 16, 16)
    return route(summed, select, incoming(piece_owner, device, 16))


def solution(mesh):
    placed = (
        P("seq", "tp", None),
        P("seq", "tp", None),
        P("seq", "tp", None),
        P("tp", None),
        P(),
        P(),
    )
    return jax.shard_map(
        on_device, mesh=mesh, in_specs=placed, out_specs=P("seq", "tp"), check_vma=False
    )
```

```python
import functools

import jax
import jax.numpy as jnp
from jax import lax
from jax.experimental import pallas as pl
from jax.experimental.pallas import tpu as pltpu
from jax.sharding import PartitionSpec as P

MASKED = -1e30
BF16, F32, I32 = jnp.bfloat16, jnp.float32, jnp.int32
ROWS = 512
HEADS = 8
HD = 128
WIDTH = 640
CHUNK = 128
CHUNKS = ROWS // CHUNK
PAIRS = HEADS // 2
GROUP = 3
SPAN = GROUP * ROWS
BACK = 8
TILES = CHUNKS * GROUP * PAIRS
FINISH = {7: 0, 13: 1, 19: 2, 25: 3}
PASS_ON = {10: 1, 13: 2, 17: 3, 20: 5, 23: 9, 25: 6, 26: 10, 27: 13, 28: 7, 29: 11, 30: 14, 31: 15}
LAST = {20: 0, 30: 1, 31: 2, 32: 3}
STEPS = 33
SCORE = HD**-0.5 * 1.4426950408889634
MESH = pl.DeviceIdType.MESH


def places():
    s = lax.axis_index("seq")
    x, z, core = s // 4, (s // 2) % 2, s % 2

    def at(step, flip_z, flip_core):
        return ((x + step) % 4) * 4 + ((z + flip_z) % 2) * 2 + (core + flip_core) % 2

    return s, z, core, at


def slot(ref_k, ref_v, delta):
    g, r = delta // GROUP, delta % GROUP
    start = pl.multiple_of(r * ROWS, ROWS)
    return (
        ref_k.at[g, pl.ds(start, ROWS), pl.ds(0, HD)],
        ref_v.at[g, pl.ds(0, HD), pl.ds(start, ROWS)],
    )


def doc_of(ends, positions):
    doc = jnp.where(positions < 0, -1, 0)
    for end in ends:
        doc = doc + jnp.where(positions >= end, 1, 0)
    return doc


def pick(index, table):
    found = -1
    for key, value in table.items():
        found = jnp.where(index == key, value, found)
    return found


def attend_kernel(
    q_ref, k_ref, v_ref, len_ref, w_hbm, o_ref,
    qx, kx, vx, acc, top, fac, diff, s0, s1, p0, p1, att, w, out_buf, ring, got_z,
    send, recv, w_sem, ring_send, ring_recv, z_send, z_recv,
):
    s, z, core, at = places()
    t = lax.axis_index("tp")
    z_lo, y = t // 4, t % 4
    sibling, next_x, prev_x, far_x, other_z = (
        at(0, 0, 1),
        at(1, 0, 0),
        at(3, 0, 0),
        at(2, 0, 0),
        at(0, 1, 0),
    )
    ahead, behind, partner = z_lo * 4 + (y + 1) % 4, z_lo * 4 + (y + 3) % 4, (1 - z_lo) * 4 + y
    load_w = pltpu.make_async_copy(w_hbm, w, w_sem)
    load_w.start()
    barrier = pltpu.get_barrier_semaphore()
    for peer in (sibling, next_x, prev_x, far_x, other_z):
        pl.semaphore_signal(barrier, inc=1, device_id={"seq": peer}, device_id_type=MESH)
    for peer in (ahead, behind, partner):
        pl.semaphore_signal(barrier, inc=1, device_id={"tp": peer}, device_id_type=MESH)

    kx[0, :ROWS, :HD] = k_ref[...]
    vx[0, :HD, :ROWS] = v_ref[...].T
    pl.semaphore_wait(barrier, 8)

    def copies(index, source, target, peer):
        for part, (a, b) in enumerate(zip(slot(kx, vx, source), slot(kx, vx, target))):
            yield pltpu.make_async_remote_copy(
                src_ref=a,
                dst_ref=b,
                send_sem=send.at[index, part],
                recv_sem=recv.at[target, part],
                device_id={"seq": peer},
                device_id_type=MESH,
            )

    def go(index, source, target, peer):
        for copy in copies(index, source, target, peer):
            copy.start()

    def arrived(target):
        for copy in copies(0, 0, target, sibling):
            copy.wait_recv()

    def to_sibling(i):
        go(4 + i, 2 * i + 2 * core, 2 * i + 1, sibling)

    def to_z(i):
        go(2 + i, 4 * z + 4 * i, 2 + 4 * i, other_z)

    go(0, 0, 4, next_x)

    @pl.when(z == 0)
    def _():
        to_z(0)

    @pl.when(core == 0)
    def _():
        to_sibling(0)

    go(1, 0, 8, far_x)

    ends = []
    total = 0
    for d in range(4):
        total = total + len_ref[d]
        ends.append(total)
    lane = lax.broadcasted_iota(I32, (ROWS, HD), 1)
    row = lax.broadcasted_iota(I32, (ROWS, HD), 0)
    mine = jnp.where(doc_of(ends, row + s * ROWS) == lane, MASKED, 0.0).astype(BF16)
    for h in range(HEADS):
        for c in range(CHUNKS):
            rows = pl.ds(c * CHUNK, CHUNK)
            place = pl.ds(h % 2 * CHUNK, CHUNK)
            qx[c, h // 2, place, :HD] = q_ref[rows, pl.ds(h * HD, HD)]
            qx[c, h // 2, place, HD:] = mine[c * CHUNK : (c + 1) * CHUNK]

    def mark(delta, _):
        start = pl.multiple_of((delta % GROUP) * ROWS, ROWS)
        seen = doc_of(ends, row + (s - delta) * ROWS) == lane
        kx[delta // GROUP, pl.ds(start, ROWS), HD:] = jnp.where(seen, 0.0, 1.0).astype(BF16)
        return 0

    lax.fori_loop(0, BACK + 1, mark, 0)
    for g in range(GROUP):
        vx[g, HD:, :] = jnp.ones((16, SPAN), BF16)
    diff[...] = lax.broadcasted_iota(I32, (ROWS, 2 * CHUNK), 0) - (
        lax.broadcasted_iota(I32, (ROWS, 2 * CHUNK), 1) % CHUNK
    )
    acc[...] = jnp.zeros_like(acc)
    fac[...] = jnp.zeros_like(fac)
    top[...] = jnp.full_like(top, MASKED)
    p1[...] = jnp.zeros_like(p1)

    arrived(4)

    @pl.when(z == 1)
    def _():
        to_z(0)

    @pl.when(z == 0)
    def _():
        to_z(1)

    @pl.when(core == 0)
    def _():
        to_sibling(2)

    @pl.when(core == 1)
    def _():
        to_sibling(1)

    arrived(2)

    @pl.when(core == 0)
    def _():
        to_sibling(1)

    @pl.when(core == 1)
    def _():
        to_sibling(0)

    arrived(1)

    scores, weights = (s0, s1), (p0, p1)

    def tile(n):
        return n // (GROUP * PAIRS), n // PAIRS % GROUP, n % PAIRS

    def score(n, out):
        c, g, p = tile(n)
        limit = c * CHUNK + g * SPAN
        qh = qx[c, p]
        both = (((1,), (1,)), ((), ()))
        near = lax.dot_general(kx[g, :ROWS, :], qh, both, preferred_element_type=F32)
        out[:ROWS] = jnp.where(diff[...] <= limit, near, MASKED)
        out[ROWS:] = lax.dot_general(kx[g, ROWS:, :], qh, both, preferred_element_type=F32)

    def weigh(n, par):
        c, g, p = tile(n)
        sc = scores[par][...]
        before = jnp.where(g == 0, MASKED, top[p, :1, :])
        now = jnp.maximum(before, jnp.max(sc, axis=0, keepdims=True))
        weights[par][...] = jnp.exp2((sc - now) * SCORE).astype(BF16)
        fac[par, :1, :] = jnp.where(g == 0, 0.0, jnp.exp2((before - now) * SCORE))
        top[p, :1, :] = now

    def mix(n, par):
        c, g, p = tile(n)
        acc[c % 2, p] = acc[c % 2, p] * fac[par, :1, :] + jnp.dot(
            vx[g], weights[par][...], preferred_element_type=F32
        )

    def ring_copy(c, k, way):
        return pltpu.make_async_remote_copy(
            src_ref=ring.at[c, k, way],
            dst_ref=ring.at[c, k + 1, way],
            send_sem=ring_send.at[c, k, way],
            recv_sem=ring_recv.at[c, k, way],
            device_id={"tp": (ahead, behind)[way]},
            device_id_type=MESH,
        )

    def z_copy(c):
        return pltpu.make_async_remote_copy(
            src_ref=ring.at[c, 3, 1 - z_lo],
            dst_ref=got_z.at[c],
            send_sem=z_send.at[c],
            recv_sem=z_recv.at[c],
            device_id={"tp": partner},
            device_id_type=MESH,
        )

    def share(c, k, way):
        owner = (y + 3 - k) % 4 if way == 0 else (y + 1 + k) % 4
        column = pl.multiple_of((way * 4 + owner) * WIDTH, HD)
        return jnp.dot(att[c], w[:, pl.ds(column, WIDTH)], preferred_element_type=F32)

    def finish(c):
        for h in range(HEADS):
            cols = pl.ds(h % 2 * CHUNK, CHUNK)
            part = acc[c % 2, h // 2, :, cols]
            value = part[:HD] / part[HD : HD + 1]
            att[c, :, pl.ds(h * HD, HD)] = value.T.astype(BF16)
        for way in range(2):
            ring[c, 0, way] = share(c, 0, way).astype(BF16)
            ring_copy(c, 0, way).start()

    def pass_on(c, k):
        for way in range(2):
            mine = share(c, k, way)
            ring_copy(c, k - 1, way).wait_recv()
            ring[c, k, way] = (ring[c, k, way].astype(F32) + mine).astype(BF16)

            @pl.when(k < 3)
            def _():
                ring_copy(c, k, way).start()

        @pl.when(k == 3)
        def _():
            z_copy(c).start()

    def last(c):
        z_copy(c).wait_recv()
        total = ring[c, 3, z_lo].astype(F32) + got_z[c].astype(F32)
        out_buf[pl.ds(pl.multiple_of(c * CHUNK, CHUNK), CHUNK), :] = total.astype(BF16)

    score(0, s0)

    def step(i, _):
        @pl.when(i == 1)
        def _():
            arrived(8)

            @pl.when(z == 1)
            def _():
                to_z(1)

            @pl.when(core == 1)
            def _():
                to_sibling(3)

            arrived(3)
            arrived(5)

        @pl.when(i == 3)
        def _():
            arrived(6)

            @pl.when(core == 0)
            def _():
                to_sibling(3)

            @pl.when(core == 1)
            def _():
                to_sibling(2)

            arrived(7)

        @pl.when(i == 7)
        def _():
            load_w.wait()

        ready = pick(i, FINISH)

        @pl.when(ready >= 0)
        def _():
            finish(ready)

        move = pick(i, PASS_ON)

        @pl.when(move >= 0)
        def _():
            pass_on(move // 4, move % 4)

        done = pick(i, LAST)

        @pl.when(done >= 0)
        def _():
            last(done)

        @pl.when(i < TILES // 2)
        def _():
            score(2 * i + 1, s1)
            weigh(2 * i, 0)
            mix(jnp.maximum(2 * i - 1, 0) + jnp.where(i == 0, PAIRS - 1, 0), 1)
            score(jnp.minimum(2 * i + 2, TILES - 1), s0)
            weigh(2 * i + 1, 1)
            mix(2 * i, 0)

        @pl.when(i == TILES // 2)
        def _():
            mix(TILES - 1, 1)

        return 0

    lax.fori_loop(0, STEPS, step, 0)
    o_ref[...] = out_buf[...]

    for index in range(4):
        for copy in copies(index, 0, 1, sibling):
            copy.wait_send()
    for i in range(4):
        for copy in copies(4 + i, 0, 1, sibling):
            copy.wait_send()
    for c in range(CHUNKS):
        for k in range(3):
            for way in range(2):
                ring_copy(c, k, way).wait_send()
        z_copy(c).wait_send()


def attention(queries, key_rows, value_rows, doc_lengths, out_weight):
    vmem = pl.BlockSpec(memory_space=pltpu.VMEM)
    return pl.pallas_call(
        attend_kernel,
        out_shape=jax.ShapeDtypeStruct((ROWS, WIDTH), BF16),
        in_specs=[
            vmem,
            vmem,
            vmem,
            pl.BlockSpec(memory_space=pltpu.SMEM),
            pl.BlockSpec(memory_space=pl.ANY),
        ],
        out_specs=vmem,
        scratch_shapes=[
            pltpu.VMEM((CHUNKS, PAIRS, 2 * CHUNK, 2 * HD), BF16),
            pltpu.VMEM((GROUP, SPAN, 2 * HD), BF16),
            pltpu.VMEM((GROUP, HD + 16, SPAN), BF16),
            pltpu.VMEM((2, PAIRS, HD + 16, 2 * CHUNK), F32),
            pltpu.VMEM((PAIRS, 8, 2 * CHUNK), F32),
            pltpu.VMEM((2, 8, 2 * CHUNK), F32),
            pltpu.VMEM((ROWS, 2 * CHUNK), I32),
            pltpu.VMEM((SPAN, 2 * CHUNK), F32),
            pltpu.VMEM((SPAN, 2 * CHUNK), F32),
            pltpu.VMEM((SPAN, 2 * CHUNK), BF16),
            pltpu.VMEM((SPAN, 2 * CHUNK), BF16),
            pltpu.VMEM((CHUNKS, CHUNK, HEADS * HD), BF16),
            pltpu.VMEM((HEADS * HD, 8 * WIDTH), BF16),
            pltpu.VMEM((ROWS, WIDTH), BF16),
            pltpu.VMEM((CHUNKS, 4, 2, CHUNK, WIDTH), BF16),
            pltpu.VMEM((CHUNKS, CHUNK, WIDTH), BF16),
            pltpu.SemaphoreType.DMA((8, 2)),
            pltpu.SemaphoreType.DMA((BACK + 1, 2)),
            pltpu.SemaphoreType.DMA,
            pltpu.SemaphoreType.DMA((CHUNKS, 3, 2)),
            pltpu.SemaphoreType.DMA((CHUNKS, 3, 2)),
            pltpu.SemaphoreType.DMA((CHUNKS,)),
            pltpu.SemaphoreType.DMA((CHUNKS,)),
        ],
        compiler_params=pltpu.CompilerParams(
            collective_id=0, has_side_effects=True, vmem_limit_bytes=56 << 20
        ),
    )(queries, key_rows, value_rows, doc_lengths, out_weight)


def outgoing(piece_owner, device, pieces, seq_count):
    local_owner = lax.dynamic_slice_in_dim(piece_owner, device * pieces, pieces)
    local_order = jnp.arange(pieces, dtype=jnp.int32)
    earlier = (local_owner[None, :] == local_owner[:, None]) & (
        local_order[None, :] < local_order[:, None]
    )
    slot_rank = jnp.sum(earlier.astype(jnp.int32), axis=1)
    target_slot = jnp.arange(seq_count * 2, dtype=jnp.int32)
    select = local_owner[None, :] * 2 + slot_rank[None, :] == target_slot[:, None]
    return select.astype(jnp.bfloat16)


def incoming(piece_owner, device, pieces):
    piece_total = piece_owner.shape[0]
    piece_ids = jnp.arange(piece_total, dtype=jnp.int32)
    is_mine = piece_owner == device
    mine_rank = jnp.cumsum(is_mine.astype(jnp.int32)) - 1
    my_slots = jnp.arange(pieces, dtype=jnp.int32)
    chosen = is_mine[None, :] & (mine_rank[None, :] == my_slots[:, None])
    held_pieces = jnp.sum(jnp.where(chosen, piece_ids[None, :], 0), axis=1)
    source_dev = held_pieces // pieces
    earlier_mine = (
        is_mine[None, :]
        & (piece_ids[None, :] // pieces == source_dev[:, None])
        & (piece_ids[None, :] < held_pieces[:, None])
    )
    slot_rank = jnp.sum(earlier_mine.astype(jnp.int32), axis=1)
    return source_dev * 2 + slot_rank


def route(row_data, select, arrival_slot):
    pieces = select.shape[1]
    row_width = row_data.shape[1]
    piece_len = row_data.shape[0] // pieces
    stacked = row_data.reshape(pieces, piece_len * row_width)
    rows = jnp.dot(select, stacked, preferred_element_type=F32).astype(row_data.dtype)
    rows = rows.reshape(select.shape[0] * piece_len, row_width)
    arrived = lax.all_to_all(rows, "seq", split_axis=0, concat_axis=0, tiled=True)
    arrived = arrived.reshape(select.shape[0], piece_len, row_width)
    return jnp.take(arrived, arrival_slot, axis=0).reshape(pieces * piece_len, row_width)


def on_device(queries, key_heads, value_heads, out_weight, doc_lengths, piece_owner):
    device = lax.axis_index("seq")
    summed = attention(
        queries.reshape(ROWS, HEADS * HD),
        key_heads.reshape(ROWS, HD),
        value_heads.reshape(ROWS, HD),
        doc_lengths,
        out_weight,
    )
    select = outgoing(piece_owner, device, 16, 16)
    return route(summed, select, incoming(piece_owner, device, 16))


def solution(mesh):
    placed = (
        P("seq", "tp", None),
        P("seq", "tp", None),
        P("seq", "tp", None),
        P("tp", None),
        P(),
        P(),
    )
    return jax.shard_map(
        on_device, mesh=mesh, in_specs=placed, out_specs=P("seq", "tp"), check_vma=False
    )
```

```python
import functools

import jax
import jax.numpy as jnp
from jax import lax
from jax.experimental import pallas as pl
from jax.experimental.pallas import tpu as pltpu
from jax.sharding import PartitionSpec as P

MASKED = -1e30
BF16, F32, I32 = jnp.bfloat16, jnp.float32, jnp.int32
ROWS = 512
HEADS = 8
HD = 128
WIDTH = 640
CHUNK = 128
CHUNKS = ROWS // CHUNK
PAIRS = HEADS // 2
GROUP = 4
SPAN = GROUP * ROWS
BACK = 8
PIECE = 32
SEQ = 16
TILES = 2 * CHUNKS * PAIRS
FINISH = {7: 0, 9: 1, 13: 2, 17: 3}
PASS_ON = {9: 1, 11: 2, 13: 5, 15: 3, 16: 6, 18: 9, 19: 7, 20: 13, 21: 10, 22: 14, 23: 11, 24: 15}
LAST = {17: 0, 21: 1, 24: 2, 25: 3}
STEPS = 26
SCORE = HD**-0.5 * 1.4426950408889634
MESH = pl.DeviceIdType.MESH


def places():
    s = lax.axis_index("seq")
    x, z, core = s // 4, (s // 2) % 2, s % 2

    def at(step, flip_z, flip_core):
        return ((x + step) % 4) * 4 + ((z + flip_z) % 2) * 2 + (core + flip_core) % 2

    return s, z, core, at


def slot(ref_k, ref_v, delta):
    g, r = (delta - 1) // GROUP, (delta - 1) % GROUP
    start = pl.multiple_of(r * ROWS, ROWS)
    return (
        ref_k.at[g, pl.ds(start, ROWS), pl.ds(0, HD)],
        ref_v.at[g, pl.ds(0, HD), pl.ds(start, ROWS)],
    )


def doc_of(ends, positions):
    doc = jnp.where(positions < 0, -1, 0)
    for end in ends:
        doc = doc + jnp.where(positions >= end, 1, 0)
    return doc


def pick(index, table):
    found = -1
    for key, value in table.items():
        found = jnp.where(index == key, value, found)
    return found


def attend_kernel(
    q_ref, k_ref, v_ref, len_ref, owner_ref, w_hbm, o_ref,
    qx, k_own, v_own, kx, vx, acc, top, fac, diff, s0, s1, p0, p1, att, w, ring, got_z,
    rows, parcels, parcels_in, out_from, in_from,
    send, recv, w_sem, ring_send, ring_recv, z_send, z_recv, parcel_send, parcel_recv,
):
    s, z, core, at = places()
    t = lax.axis_index("tp")
    z_lo, y = t // 4, t % 4
    sibling, next_x, prev_x, far_x, other_z = (
        at(0, 0, 1),
        at(1, 0, 0),
        at(3, 0, 0),
        at(2, 0, 0),
        at(0, 1, 0),
    )
    ahead, behind, partner = z_lo * 4 + (y + 1) % 4, z_lo * 4 + (y + 3) % 4, (1 - z_lo) * 4 + y
    load_w = pltpu.make_async_copy(w_hbm, w, w_sem)
    load_w.start()
    barrier = pltpu.get_barrier_semaphore()
    for k in range(1, SEQ):
        pl.semaphore_signal(
            barrier, inc=1, device_id={"seq": (s + k) % SEQ}, device_id_type=MESH
        )
    for peer in (ahead, behind, partner):
        pl.semaphore_signal(barrier, inc=1, device_id={"tp": peer}, device_id_type=MESH)

    k_own[:, :HD] = k_ref[...]
    v_own[:HD] = v_ref[...].T
    pl.semaphore_wait(barrier, SEQ - 1 + 3)

    def copy_of(index, source, target, peer, part):
        if source is None:
            a = (k_own.at[:, pl.ds(0, HD)], v_own.at[pl.ds(0, HD), :])[part]
        else:
            a = slot(kx, vx, source)[part]
        return pltpu.make_async_remote_copy(
            src_ref=a,
            dst_ref=slot(kx, vx, target)[part],
            send_sem=send.at[index, part],
            recv_sem=recv.at[target, part],
            device_id={"seq": peer},
            device_id_type=MESH,
        )

    def copies(index, source, target, peer):
        return [copy_of(index, source, target, peer, part) for part in range(2)]

    def go(index, source, target, peer, part):
        copy_of(index, source, target, peer, part).start()

    def arrived(target, part):
        copy_of(0, None, target, sibling, part).wait_recv()

    def pass_block(name, part):
        if name == 4:
            @pl.when(z == 1)
            def _():
                go(2, 4, 2, other_z, part)

            @pl.when(z == 0)
            def _():
                go(3, 4, 6, other_z, part)

        if name == 8:
            @pl.when(z == 1)
            def _():
                go(3, 8, 6, other_z, part)

        if name < 8:
            @pl.when(core == 0)
            def _():
                go(4 + name // 2, name, name + 1, sibling, part)

        @pl.when(core == 1)
        def _():
            go(3 + name // 2, name, name - 1, sibling, part)

    for part in range(2):
        go(0, None, 4, next_x, part)

        @pl.when(z == 0)
        def _():
            go(2, None, 2, other_z, part)

        @pl.when(core == 0)
        def _():
            go(4, None, 1, sibling, part)

    ends = []
    total = 0
    for d in range(4):
        total = total + len_ref[d]
        ends.append(total)
    lane = lax.broadcasted_iota(I32, (ROWS, HD), 1)
    row = lax.broadcasted_iota(I32, (ROWS, HD), 0)
    mine = jnp.where(doc_of(ends, row + s * ROWS) == lane, MASKED, 0.0).astype(BF16)
    for h in range(HEADS):
        for c in range(CHUNKS):
            queries = pl.ds(c * CHUNK, CHUNK)
            side = pl.ds(h % 2 * CHUNK, CHUNK)
            qx[c, h // 2, side, :HD] = q_ref[queries, pl.ds(h * HD, HD)]
            qx[c, h // 2, side, HD:] = mine[c * CHUNK : (c + 1) * CHUNK]

    own_seen = doc_of(ends, row + s * ROWS) == lane
    k_own[:, HD:] = jnp.where(own_seen, 0.0, 1.0).astype(BF16)
    v_own[HD:] = jnp.ones((16, ROWS), BF16)

    def mark(delta, _):
        start = pl.multiple_of((delta - 1) % GROUP * ROWS, ROWS)
        seen = doc_of(ends, row + (s - delta) * ROWS) == lane
        kx[(delta - 1) // GROUP, pl.ds(start, ROWS), HD:] = jnp.where(seen, 0.0, 1.0).astype(BF16)
        return 0

    lax.fori_loop(1, BACK + 1, mark, 0)
    for g in range(2):
        vx[g, HD:, :] = jnp.ones((16, SPAN), BF16)
    diff[...] = lax.broadcasted_iota(I32, (ROWS, 2 * CHUNK), 0) - (
        lax.broadcasted_iota(I32, (ROWS, 2 * CHUNK), 1) % CHUNK
    )
    fac[...] = jnp.ones_like(fac)
    p1[...] = jnp.zeros_like(p1)

    scores, weights = (s0, s1), (p0, p1)

    both = (((1,), (1,)), ((), ()))

    def own_pass(i, _):
        @pl.when(i == 3)
        def _():
            arrived(4, 0)
            pass_block(4, 0)

        @pl.when(i == 5)
        def _():
            arrived(4, 1)
            pass_block(4, 1)

        c = i // 2
        pairs = (i % 2 * 2, i % 2 * 2 + 1)
        for par, p in enumerate(pairs):
            near = lax.dot_general(k_own[...], qx[c, p], both, preferred_element_type=F32)
            scores[par][:ROWS] = jnp.where(diff[...] <= c * CHUNK, near, MASKED)
        for par, p in enumerate(pairs):
            sc = scores[par][:ROWS]
            now = jnp.max(sc, axis=0, keepdims=True)
            top[c, p, :1, :] = now
            weight = jnp.exp2((sc - now) * SCORE).astype(BF16)
            acc[c, p] = jnp.dot(v_own[...], weight, preferred_element_type=F32)
        return 0

    lax.fori_loop(0, 2 * CHUNKS, own_pass, 0)

    for part in range(2):
        copy_of(0, None, 4, next_x, part).wait_send()
        go(1, None, 8, far_x, part)

    own = [owner_ref[s * 16 + k] for k in range(16)]
    place = []
    for k in range(16):
        rank = 0
        for j in range(k):
            rank = rank + jnp.where(own[j] == own[k], 1, 0)
        place.append(2 * own[k] + rank)
    for n in range(2 * SEQ):
        piece = 0
        for k in range(16):
            piece = piece + jnp.where(place[k] == n, k, 0)
        out_from[n] = piece
    before = 0
    found = [0] * 16
    for source in range(SEQ):
        count = 0
        for k in range(16):
            count = count + jnp.where(owner_ref[source * 16 + k] == s, 1, 0)
        far = (s - source + SEQ) % SEQ
        for j in range(16):
            for r in range(2):
                hit = (before + r == j) & (r < count)
                found[j] = found[j] + jnp.where(hit, 2 * far + r, 0)
        before = before + count
    for j in range(16):
        in_from[j] = found[j]

    for part in range(2):
        arrived(2, part)
        pass_block(2, part)
    for part in range(2):
        arrived(1, part)
        arrived(3, part)

    def tile(n):
        b = n // PAIRS
        c = jnp.where(b < 4, b % 2, b // 2)
        g = jnp.where(b < 4, b // 2, b % 2)
        return c, g, n % PAIRS

    def score(n, out):
        c, g, p = tile(n)
        out[...] = lax.dot_general(kx[g], qx[c, p], both, preferred_element_type=F32)

    def weigh(n, par):
        c, g, p = tile(n)
        sc = scores[par][...]
        before = top[c, p, :1, :]
        now = jnp.maximum(before, jnp.max(sc, axis=0, keepdims=True))
        weights[par][...] = jnp.exp2((sc - now) * SCORE).astype(BF16)
        fac[par, :1, :] = jnp.exp2((before - now) * SCORE)
        top[c, p, :1, :] = now

    def mix(n, par):
        c, g, p = tile(n)
        acc[c, p] = acc[c, p] * fac[par, :1, :] + jnp.dot(
            vx[g], weights[par][...], preferred_element_type=F32
        )

    def ring_copy(c, k, way):
        return pltpu.make_async_remote_copy(
            src_ref=ring.at[c, k, way],
            dst_ref=ring.at[c, k + 1, way],
            send_sem=ring_send.at[c, k, way],
            recv_sem=ring_recv.at[c, k, way],
            device_id={"tp": (ahead, behind)[way]},
            device_id_type=MESH,
        )

    def z_copy(c):
        return pltpu.make_async_remote_copy(
            src_ref=ring.at[c, 3, 1 - z_lo],
            dst_ref=got_z.at[c],
            send_sem=z_send.at[c],
            recv_sem=z_recv.at[c],
            device_id={"tp": partner},
            device_id_type=MESH,
        )

    def share(c, k, way):
        owner = (y + 3 - k) % 4 if way == 0 else (y + 1 + k) % 4
        column = pl.multiple_of((way * 4 + owner) * WIDTH, HD)
        return jnp.dot(att[c], w[:, pl.ds(column, WIDTH)], preferred_element_type=F32)

    def finish(c):
        for h in range(HEADS):
            cols = pl.ds(h % 2 * CHUNK, CHUNK)
            part = acc[c, h // 2, :, cols]
            value = part[:HD] / part[HD : HD + 1]
            att[c, :, pl.ds(h * HD, HD)] = value.T.astype(BF16)
        for way in range(2):
            ring[c, 0, way] = share(c, 0, way).astype(BF16)
            ring_copy(c, 0, way).start()

    def pass_on(c, k):
        for way in range(2):
            mine = share(c, k, way)
            ring_copy(c, k - 1, way).wait_recv()
            ring[c, k, way] = (ring[c, k, way].astype(F32) + mine).astype(BF16)

            @pl.when(k < 3)
            def _():
                ring_copy(c, k, way).start()

        @pl.when(k == 3)
        def _():
            z_copy(c).start()

    def last(c):
        z_copy(c).wait_recv()
        total = ring[c, 3, z_lo].astype(F32) + got_z[c].astype(F32)
        rows[pl.ds(c * 4, 4)] = total.astype(BF16).reshape(4, PIECE, WIDTH)

    score(0, s0)

    def step(i, _):
        @pl.when(i == 1)
        def _():
            for part in range(2):
                arrived(8, part)
                pass_block(8, part)

        @pl.when(i == 3)
        def _():
            for part in range(2):
                arrived(6, part)
                pass_block(6, part)
            for part in range(2):
                arrived(5, part)
                arrived(7, part)

        @pl.when(i == 7)
        def _():
            load_w.wait()

        ready = pick(i, FINISH)

        @pl.when(ready >= 0)
        def _():
            finish(ready)

        move = pick(i, PASS_ON)

        @pl.when(move >= 0)
        def _():
            pass_on(move // 4, move % 4)

        done = pick(i, LAST)

        @pl.when(done >= 0)
        def _():
            last(done)

        @pl.when(i < TILES // 2)
        def _():
            score(2 * i + 1, s1)
            weigh(2 * i, 0)
            mix(jnp.maximum(2 * i - 1, 0), 1)
            score(jnp.minimum(2 * i + 2, TILES - 1), s0)
            weigh(2 * i + 1, 1)
            mix(2 * i, 0)

        @pl.when(i == TILES // 2)
        def _():
            mix(TILES - 1, 1)

        return 0

    lax.fori_loop(0, STEPS, step, 0)

    def parcel(k):
        return pltpu.make_async_remote_copy(
            src_ref=parcels.at[k],
            dst_ref=parcels_in.at[k],
            send_sem=parcel_send.at[k],
            recv_sem=parcel_recv.at[k],
            device_id={"seq": (s + k) % SEQ},
            device_id_type=MESH,
        )

    for k in range(1, SEQ):
        for r in range(2):
            parcels[k, r] = rows[out_from[(s + k) % SEQ * 2 + r]]
        parcel(k).start()
    for r in range(2):
        parcels_in[0, r] = rows[out_from[s * 2 + r]]
    for k in range(1, SEQ):
        parcel(k).wait_recv()
    for j in range(16):
        n = in_from[j]
        o_ref[pl.ds(j * PIECE, PIECE), :] = parcels_in[n // 2, n % 2]
    for k in range(1, SEQ):
        parcel(k).wait_send()

    for index in range(1, 4):
        for copy in copies(index, 1, 1, sibling):
            copy.wait_send()
    for i in range(4):
        for copy in copies(4 + i, 1, 1, sibling):
            copy.wait_send()
    for c in range(CHUNKS):
        for k in range(3):
            for way in range(2):
                ring_copy(c, k, way).wait_send()
        z_copy(c).wait_send()


def attention(queries, key_rows, value_rows, doc_lengths, piece_owner, out_weight):
    vmem = pl.BlockSpec(memory_space=pltpu.VMEM)
    return pl.pallas_call(
        attend_kernel,
        out_shape=jax.ShapeDtypeStruct((ROWS, WIDTH), BF16),
        in_specs=[
            vmem,
            vmem,
            vmem,
            pl.BlockSpec(memory_space=pltpu.SMEM),
            pl.BlockSpec(memory_space=pltpu.SMEM),
            pl.BlockSpec(memory_space=pl.ANY),
        ],
        out_specs=vmem,
        scratch_shapes=[
            pltpu.VMEM((CHUNKS, PAIRS, 2 * CHUNK, 2 * HD), BF16),
            pltpu.VMEM((ROWS, 2 * HD), BF16),
            pltpu.VMEM((HD + 16, ROWS), BF16),
            pltpu.VMEM((2, SPAN, 2 * HD), BF16),
            pltpu.VMEM((2, HD + 16, SPAN), BF16),
            pltpu.VMEM((CHUNKS, PAIRS, HD + 16, 2 * CHUNK), F32),
            pltpu.VMEM((CHUNKS, PAIRS, 8, 2 * CHUNK), F32),
            pltpu.VMEM((2, 8, 2 * CHUNK), F32),
            pltpu.VMEM((ROWS, 2 * CHUNK), I32),
            pltpu.VMEM((SPAN, 2 * CHUNK), F32),
            pltpu.VMEM((SPAN, 2 * CHUNK), F32),
            pltpu.VMEM((SPAN, 2 * CHUNK), BF16),
            pltpu.VMEM((SPAN, 2 * CHUNK), BF16),
            pltpu.VMEM((CHUNKS, CHUNK, HEADS * HD), BF16),
            pltpu.VMEM((HEADS * HD, 8 * WIDTH), BF16),
            pltpu.VMEM((CHUNKS, 4, 2, CHUNK, WIDTH), BF16),
            pltpu.VMEM((CHUNKS, CHUNK, WIDTH), BF16),
            pltpu.VMEM((16, PIECE, WIDTH), BF16),
            pltpu.VMEM((SEQ, 2, PIECE, WIDTH), BF16),
            pltpu.VMEM((SEQ, 2, PIECE, WIDTH), BF16),
            pltpu.SMEM((2 * SEQ,), I32),
            pltpu.SMEM((16,), I32),
            pltpu.SemaphoreType.DMA((8, 2)),
            pltpu.SemaphoreType.DMA((BACK + 1, 2)),
            pltpu.SemaphoreType.DMA,
            pltpu.SemaphoreType.DMA((CHUNKS, 3, 2)),
            pltpu.SemaphoreType.DMA((CHUNKS, 3, 2)),
            pltpu.SemaphoreType.DMA((CHUNKS,)),
            pltpu.SemaphoreType.DMA((CHUNKS,)),
            pltpu.SemaphoreType.DMA((SEQ,)),
            pltpu.SemaphoreType.DMA((SEQ,)),
        ],
        compiler_params=pltpu.CompilerParams(
            collective_id=0, has_side_effects=True, vmem_limit_bytes=56 << 20
        ),
    )(queries, key_rows, value_rows, doc_lengths, piece_owner, out_weight)


def on_device(queries, key_heads, value_heads, out_weight, doc_lengths, piece_owner):
    return attention(
        queries.reshape(ROWS, HEADS * HD),
        key_heads.reshape(ROWS, HD),
        value_heads.reshape(ROWS, HD),
        doc_lengths,
        piece_owner,
        out_weight,
    )


def solution(mesh):
    placed = (
        P("seq", "tp", None),
        P("seq", "tp", None),
        P("seq", "tp", None),
        P("tp", None),
        P(),
        P(),
    )
    return jax.shard_map(
        on_device, mesh=mesh, in_specs=placed, out_specs=P("seq", "tp"), check_vma=False
    )
```

```python
import functools

import jax
import jax.numpy as jnp
from jax import lax
from jax.experimental import pallas as pl
from jax.experimental.pallas import tpu as pltpu
from jax.sharding import PartitionSpec as P

MASKED = -1e30
BF16, F32, I32 = jnp.bfloat16, jnp.float32, jnp.int32
ROWS = 512
HEADS = 8
HD = 128
WIDTH = 640
CHUNK = 128
CHUNKS = ROWS // CHUNK
PAIRS = HEADS // 2
GROUP = 4
SPAN = GROUP * ROWS
BACK = 8
PIECE = 32
SEQ = 16
TILES = 2 * CHUNKS * PAIRS
SLICES = ((0, 384), (384, 256))
FINISH = {5: 0, 9: 1, 13: 2, 17: 3}
PASS_ON = (
    {5: 4, 7: 1, 8: 5, 9: 2, 11: 9, 12: 3, 13: 7, 14: 17, 16: 11, 17: 14, 18: 18, 19: 21, 20: 25, 21: 15, 22: 28, 23: 19, 24: 22, 25: 26, 26: 29, 27: 23, 28: 27, 29: 30, 30: 31},
    {9: 6, 13: 10, 14: 20},
    {9: 12, 13: 13},
)
LAST = {13: 0, 15: 1, 20: 2, 25: 3, 26: 4, 30: 5, 31: 6, 32: 7}
ROUTE = {31: 0, 32: 1}
PLACES = 15
STEPS = 33
SCORE = HD**-0.5 * 1.4426950408889634
MESH = pl.DeviceIdType.MESH


def places():
    s = lax.axis_index("seq")
    x, z, core = s // 4, (s // 2) % 2, s % 2

    def at(step, flip_z, flip_core):
        return ((x + step) % 4) * 4 + ((z + flip_z) % 2) * 2 + (core + flip_core) % 2

    return s, z, core, at


def slot(ref_k, ref_v, delta):
    g, r = (delta - 1) // GROUP, (delta - 1) % GROUP
    start = pl.multiple_of(r * ROWS, ROWS)
    return (
        ref_k.at[g, pl.ds(start, ROWS), pl.ds(0, HD)],
        ref_v.at[g, pl.ds(0, HD), pl.ds(start, ROWS)],
    )


def doc_of(ends, positions):
    doc = jnp.where(positions < 0, -1, 0)
    for end in ends:
        doc = doc + jnp.where(positions >= end, 1, 0)
    return doc


def pick(index, table):
    found = -1
    for key, value in table.items():
        found = jnp.where(index == key, value, found)
    return found


def attend_kernel(
    q_ref, k_ref, v_ref, len_ref, owner_ref, w_hbm, o_ref,
    qx, k_own, v_own, kx, vx, acc, top, fac, diff, s0, s1, p0, p1, att, w, parts,
    ring0, ring1, got0, got1, rows0, rows1, parcels0, parcels1, in0, in1, out_from, in_from,
    send, recv, w_sem, ring_send, ring_recv, z_send, z_recv, parcel_send, parcel_recv,
):
    ring, got_z, rows, parcels, parcels_in = (
        (ring0, ring1),
        (got0, got1),
        (rows0, rows1),
        (parcels0, parcels1),
        (in0, in1),
    )
    s, z, core, at = places()
    t = lax.axis_index("tp")
    z_lo, y = t // 4, t % 4
    sibling, next_x, prev_x, far_x, other_z = (
        at(0, 0, 1),
        at(1, 0, 0),
        at(3, 0, 0),
        at(2, 0, 0),
        at(0, 1, 0),
    )
    ahead, behind, partner = z_lo * 4 + (y + 1) % 4, z_lo * 4 + (y + 3) % 4, (1 - z_lo) * 4 + y
    load_w = pltpu.make_async_copy(w_hbm, w, w_sem)
    load_w.start()
    barrier = pltpu.get_barrier_semaphore()
    for k in range(1, SEQ):
        pl.semaphore_signal(
            barrier, inc=1, device_id={"seq": (s + k) % SEQ}, device_id_type=MESH
        )
    for peer in (ahead, behind, partner):
        pl.semaphore_signal(barrier, inc=1, device_id={"tp": peer}, device_id_type=MESH)

    k_own[:, :HD] = k_ref[...]
    v_own[:HD] = v_ref[...].T
    pl.semaphore_wait(barrier, SEQ - 1 + 3)

    def copy_of(index, source, target, peer, part):
        if source is None:
            a = (k_own.at[:, pl.ds(0, HD)], v_own.at[pl.ds(0, HD), :])[part]
        else:
            a = slot(kx, vx, source)[part]
        return pltpu.make_async_remote_copy(
            src_ref=a,
            dst_ref=slot(kx, vx, target)[part],
            send_sem=send.at[index, part],
            recv_sem=recv.at[target, part],
            device_id={"seq": peer},
            device_id_type=MESH,
        )

    def copies(index, source, target, peer):
        return [copy_of(index, source, target, peer, part) for part in range(2)]

    def go(index, source, target, peer, part):
        copy_of(index, source, target, peer, part).start()

    def arrived(target, part):
        copy_of(0, None, target, sibling, part).wait_recv()

    def pass_block(name, part):
        if name == 4:
            @pl.when(z == 1)
            def _():
                go(2, 4, 2, other_z, part)

            @pl.when(z == 0)
            def _():
                go(3, 4, 6, other_z, part)

        if name == 8:
            @pl.when(z == 1)
            def _():
                go(3, 8, 6, other_z, part)

        if name < 8:
            @pl.when(core == 0)
            def _():
                go(4 + name // 2, name, name + 1, sibling, part)

        @pl.when(core == 1)
        def _():
            go(3 + name // 2, name, name - 1, sibling, part)

    for part in range(2):
        go(0, None, 4, next_x, part)

        @pl.when(z == 0)
        def _():
            go(2, None, 2, other_z, part)

        @pl.when(core == 0)
        def _():
            go(4, None, 1, sibling, part)

    for part in range(2):
        go(1, None, 8, far_x, part)

    ends = []
    total = 0
    for d in range(4):
        total = total + len_ref[d]
        ends.append(total)
    lane = lax.broadcasted_iota(I32, (ROWS, HD), 1)
    row = lax.broadcasted_iota(I32, (ROWS, HD), 0)
    mine = jnp.where(doc_of(ends, row + s * ROWS) == lane, MASKED, 0.0).astype(BF16)
    for h in range(HEADS):
        for c in range(CHUNKS):
            queries = pl.ds(c * CHUNK, CHUNK)
            side = pl.ds(h % 2 * CHUNK, CHUNK)
            qx[c, h // 2, side, :HD] = q_ref[queries, h, :]
            qx[c, h // 2, side, HD:] = mine[c * CHUNK : (c + 1) * CHUNK]

    own_seen = doc_of(ends, row + s * ROWS) == lane
    k_own[:, HD:] = jnp.where(own_seen, 0.0, 1.0).astype(BF16)
    v_own[HD:] = jnp.ones((16, ROWS), BF16)

    diff[...] = lax.broadcasted_iota(I32, (ROWS, 2 * CHUNK), 0) - (
        lax.broadcasted_iota(I32, (ROWS, 2 * CHUNK), 1) % CHUNK
    )
    fac[...] = jnp.ones_like(fac)
    p1[...] = jnp.zeros_like(p1)

    scores, weights = (s0, s1), (p0, p1)

    both = (((1,), (1,)), ((), ()))

    def own_pass(i, _):
        @pl.when(i == 3)
        def _():
            arrived(4, 0)
            pass_block(4, 0)

        @pl.when(i == 5)
        def _():
            arrived(4, 1)
            pass_block(4, 1)

        c = i // 2
        pairs = (i % 2 * 2, i % 2 * 2 + 1)
        for par, p in enumerate(pairs):
            near = lax.dot_general(k_own[...], qx[c, p], both, preferred_element_type=F32)
            scores[par][:ROWS] = jnp.where(diff[...] <= c * CHUNK, near, MASKED)
        for par, p in enumerate(pairs):
            sc = scores[par][:ROWS]
            now = jnp.max(sc, axis=0, keepdims=True)
            top[c, p, :1, :] = now
            weight = jnp.exp2((sc - now) * SCORE).astype(BF16)
            acc[c, p] = jnp.dot(v_own[...], weight, preferred_element_type=F32)
        return 0

    lax.fori_loop(0, 2 * CHUNKS, own_pass, 0)

    def mark(delta, _):
        start = pl.multiple_of((delta - 1) % GROUP * ROWS, ROWS)
        seen = doc_of(ends, row + (s - delta) * ROWS) == lane
        kx[(delta - 1) // GROUP, pl.ds(start, ROWS), HD:] = jnp.where(seen, 0.0, 1.0).astype(BF16)
        return 0

    lax.fori_loop(1, BACK + 1, mark, 0)
    for g in range(2):
        vx[g, HD:, :] = jnp.ones((16, SPAN), BF16)
    for name in (2, 8):
        for part in range(2):
            arrived(name, part)
            pass_block(name, part)
    for part in range(2):
        arrived(1, part)
        arrived(3, part)

    def tile(n):
        b = n // PAIRS
        return b // 2, b % 2, n % PAIRS

    def score(n, out):
        c, g, p = tile(n)
        out[...] = lax.dot_general(kx[g], qx[c, p], both, preferred_element_type=F32)

    def weigh(n, par):
        c, g, p = tile(n)
        sc = scores[par][...]
        before = top[c, p, :1, :]
        now = jnp.maximum(before, jnp.max(sc, axis=0, keepdims=True))
        weights[par][...] = jnp.exp2((sc - now) * SCORE).astype(BF16)
        fac[par, :1, :] = jnp.exp2((before - now) * SCORE)
        top[c, p, :1, :] = now

    def mix(n, par):
        c, g, p = tile(n)
        acc[c, p] = acc[c, p] * fac[par, :1, :] + jnp.dot(
            vx[g], weights[par][...], preferred_element_type=F32
        )

    def ring_copy(j, c, k, way):
        return pltpu.make_async_remote_copy(
            src_ref=ring[j].at[c, k, way],
            dst_ref=ring[j].at[c, k + 1, way],
            send_sem=ring_send.at[j, c, k, way],
            recv_sem=ring_recv.at[j, c, k, way],
            device_id={"tp": (ahead, behind)[way]},
            device_id_type=MESH,
        )

    def z_copy(j, c):
        return pltpu.make_async_remote_copy(
            src_ref=ring[j].at[c, 3, 1 - z_lo],
            dst_ref=got_z[j].at[c],
            send_sem=z_send.at[j, c],
            recv_sem=z_recv.at[j, c],
            device_id={"tp": partner},
            device_id_type=MESH,
        )

    def share(c, k, way):
        owner = (y + 3 - k) % 4 if way == 0 else (y + 1 + k) % 4
        column = pl.multiple_of((way * 4 + owner) * WIDTH, HD)
        return jnp.dot(att[c], w[:, pl.ds(column, WIDTH)], preferred_element_type=F32)

    def finish(c):
        for h in range(HEADS):
            cols = pl.ds(h % 2 * CHUNK, CHUNK)
            part = acc[c, h // 2, :, cols]
            value = part[:HD] / part[HD : HD + 1]
            att[c, :, pl.ds(h * HD, HD)] = value.T.astype(BF16)
        for way in range(2):
            first = share(c, 0, way).astype(BF16)
            for j, (column, width) in enumerate(SLICES):
                ring[j][c, 0, way] = first[:, column : column + width]
            ring_copy(0, c, 0, way).start()

        def others(k, _):
            for way in range(2):
                parts[c, k - 1, way] = share(c, k, way)
            return 0

        lax.fori_loop(1, 4, others, 0)

    def pass_on(j, c, k):
        column, width = SLICES[j]

        @pl.when(k > 0)
        def _():
            for way in range(2):
                ring_copy(j, c, k - 1, way).wait_recv()
                mine = parts[c, k - 1, way, :, column : column + width]
                ring[j][c, k, way] = (ring[j][c, k, way].astype(F32) + mine).astype(BF16)

        @pl.when(k < 3)
        def _():
            for way in range(2):
                ring_copy(j, c, k, way).start()

        @pl.when(k == 3)
        def _():
            z_copy(j, c).start()

    def last(j, c):
        z_copy(j, c).wait_recv()
        total = ring[j][c, 3, z_lo].astype(F32) + got_z[j][c].astype(F32)
        rows[j][pl.ds(c * 4, 4)] = total.astype(BF16).reshape(4, PIECE, SLICES[j][1])

    def parcel(j, k):
        return pltpu.make_async_remote_copy(
            src_ref=parcels[j].at[k],
            dst_ref=parcels_in[j].at[k],
            send_sem=parcel_send.at[j, k],
            recv_sem=parcel_recv.at[j, k],
            device_id={"seq": (s + k) % SEQ},
            device_id_type=MESH,
        )

    def route(j):
        for k in range(1, SEQ):
            for r in range(2):
                parcels[j][k, r] = rows[j][out_from[(s + k) % SEQ * 2 + r]]
            parcel(j, k).start()
        for r in range(2):
            parcels_in[j][0, r] = rows[j][out_from[s * 2 + r]]

    score(0, s0)

    def step(i, _):
        @pl.when(i == 1)
        def _():
            for part in range(2):
                arrived(6, part)
                pass_block(6, part)
            for part in range(2):
                arrived(5, part)
                arrived(7, part)

        @pl.when(i == 5)
        def _():
            load_w.wait()

        @pl.when(i == PLACES)
        def _():
            own = [owner_ref[s * 16 + k] for k in range(16)]
            place = []
            for k in range(16):
                rank = 0
                for j in range(k):
                    rank = rank + jnp.where(own[j] == own[k], 1, 0)
                place.append(2 * own[k] + rank)
            for n in range(2 * SEQ):
                piece = 0
                for k in range(16):
                    piece = piece + jnp.where(place[k] == n, k, 0)
                out_from[n] = piece
            before = 0
            found = [0] * 16
            for source in range(SEQ):
                count = 0
                for k in range(16):
                    count = count + jnp.where(owner_ref[source * 16 + k] == s, 1, 0)
                far = (s - source + SEQ) % SEQ
                for j in range(16):
                    for r in range(2):
                        hit = (before + r == j) & (r < count)
                        found[j] = found[j] + jnp.where(hit, 2 * far + r, 0)
                before = before + count
            for j in range(16):
                in_from[j] = found[j]

        ready = pick(i, FINISH)

        @pl.when(ready >= 0)
        def _():
            finish(ready)

        for table in PASS_ON:
            move = pick(i, table)
            for j in range(2):

                @pl.when((move >= 0) & (move // 4 % 2 == j))
                def _(j=j):
                    pass_on(j, move // 8, move % 4)

        done = pick(i, LAST)
        leave = pick(i, ROUTE)
        for j in range(2):

            @pl.when((done >= 0) & (done % 2 == j))
            def _(j=j):
                last(j, done // 2)

            @pl.when(leave == j)
            def _(j=j):
                route(j)

        @pl.when(i < TILES // 2)
        def _():
            score(2 * i + 1, s1)
            weigh(2 * i, 0)
            mix(jnp.maximum(2 * i - 1, 0), 1)
            score(jnp.minimum(2 * i + 2, TILES - 1), s0)
            weigh(2 * i + 1, 1)
            mix(2 * i, 0)

        @pl.when(i == TILES // 2)
        def _():
            mix(TILES - 1, 1)

        return 0

    lax.fori_loop(0, STEPS, step, 0)

    for j, (column, width) in enumerate(SLICES):
        for k in range(1, SEQ):
            parcel(j, k).wait_recv()
        for k in range(16):
            n = in_from[k]
            o_ref[pl.ds(k * PIECE, PIECE), column : column + width] = parcels_in[j][n // 2, n % 2]
    for j in range(2):
        for k in range(1, SEQ):
            parcel(j, k).wait_send()

    for index in range(4):
        for copy in copies(index, 1, 1, sibling):
            copy.wait_send()
    for i in range(4):
        for copy in copies(4 + i, 1, 1, sibling):
            copy.wait_send()
    for j in range(2):
        for c in range(CHUNKS):
            for k in range(3):
                for way in range(2):
                    ring_copy(j, c, k, way).wait_send()
            z_copy(j, c).wait_send()


def attention(queries, key_rows, value_rows, doc_lengths, piece_owner, out_weight):
    vmem = pl.BlockSpec(memory_space=pltpu.VMEM)
    return pl.pallas_call(
        attend_kernel,
        out_shape=jax.ShapeDtypeStruct((ROWS, WIDTH), BF16),
        in_specs=[
            vmem,
            vmem,
            vmem,
            pl.BlockSpec(memory_space=pltpu.SMEM),
            pl.BlockSpec(memory_space=pltpu.SMEM),
            pl.BlockSpec(memory_space=pl.ANY),
        ],
        out_specs=vmem,
        scratch_shapes=[
            pltpu.VMEM((CHUNKS, PAIRS, 2 * CHUNK, 2 * HD), BF16),
            pltpu.VMEM((ROWS, 2 * HD), BF16),
            pltpu.VMEM((HD + 16, ROWS), BF16),
            pltpu.VMEM((2, SPAN, 2 * HD), BF16),
            pltpu.VMEM((2, HD + 16, SPAN), BF16),
            pltpu.VMEM((CHUNKS, PAIRS, HD + 16, 2 * CHUNK), F32),
            pltpu.VMEM((CHUNKS, PAIRS, 8, 2 * CHUNK), F32),
            pltpu.VMEM((2, 8, 2 * CHUNK), F32),
            pltpu.VMEM((ROWS, 2 * CHUNK), I32),
            pltpu.VMEM((SPAN, 2 * CHUNK), F32),
            pltpu.VMEM((SPAN, 2 * CHUNK), F32),
            pltpu.VMEM((SPAN, 2 * CHUNK), BF16),
            pltpu.VMEM((SPAN, 2 * CHUNK), BF16),
            pltpu.VMEM((CHUNKS, CHUNK, HEADS * HD), BF16),
            pltpu.VMEM((HEADS * HD, 8 * WIDTH), BF16),
            pltpu.VMEM((CHUNKS, 3, 2, CHUNK, WIDTH), F32),
            *(pltpu.VMEM((CHUNKS, 4, 2, CHUNK, width), BF16) for _, width in SLICES),
            *(pltpu.VMEM((CHUNKS, CHUNK, width), BF16) for _, width in SLICES),
            *(pltpu.VMEM((16, PIECE, width), BF16) for _, width in SLICES),
            *(pltpu.VMEM((SEQ, 2, PIECE, width), BF16) for _, width in SLICES),
            *(pltpu.VMEM((SEQ, 2, PIECE, width), BF16) for _, width in SLICES),
            pltpu.SMEM((2 * SEQ,), I32),
            pltpu.SMEM((16,), I32),
            pltpu.SemaphoreType.DMA((8, 2)),
            pltpu.SemaphoreType.DMA((BACK + 1, 2)),
            pltpu.SemaphoreType.DMA,
            pltpu.SemaphoreType.DMA((2, CHUNKS, 3, 2)),
            pltpu.SemaphoreType.DMA((2, CHUNKS, 3, 2)),
            pltpu.SemaphoreType.DMA((2, CHUNKS)),
            pltpu.SemaphoreType.DMA((2, CHUNKS)),
            pltpu.SemaphoreType.DMA((2, SEQ)),
            pltpu.SemaphoreType.DMA((2, SEQ)),
        ],
        compiler_params=pltpu.CompilerParams(
            collective_id=0, has_side_effects=True, vmem_limit_bytes=56 << 20
        ),
    )(queries, key_rows, value_rows, doc_lengths, piece_owner, out_weight)


def on_device(queries, key_heads, value_heads, out_weight, doc_lengths, piece_owner):
    return attention(
        queries,
        key_heads.reshape(ROWS, HD),
        value_heads.reshape(ROWS, HD),
        doc_lengths,
        piece_owner,
        out_weight,
    )


def solution(mesh):
    placed = (
        P("seq", "tp", None),
        P("seq", "tp", None),
        P("seq", "tp", None),
        P("tp", None),
        P(),
        P(),
    )
    return jax.shard_map(
        on_device, mesh=mesh, in_specs=placed, out_specs=P("seq", "tp"), check_vma=False
    )
```

```python
import functools

import jax
import jax.numpy as jnp
from jax import lax
from jax.experimental import pallas as pl
from jax.experimental.pallas import tpu as pltpu
from jax.sharding import PartitionSpec as P

MASKED = -1e30
BF16, F32, I32 = jnp.bfloat16, jnp.float32, jnp.int32
ROWS = 512
HEADS = 8
HD = 128
WIDTH = 640
CHUNK = 128
CHUNKS = ROWS // CHUNK
PAIRS = HEADS // 2
GROUP = 4
SPAN = GROUP * ROWS
BACK = 8
PIECE = 32
SEQ = 16
TILES = 2 * CHUNKS * PAIRS
SLICES = ((0, 256), (256, 256), (512, 128))
PARTS = len(SLICES)
LATE = ((2, 2), (3, 2))
FINISH = {5: 0, 9: 1, 13: 2, 17: 3}
SHARE = {6: 1, 7: 2, 8: 3, 10: 5, 11: 6, 12: 7, 14: 9, 15: 10, 16: 11, 18: 13, 19: 14, 20: 15}
PASS_ON = (
    {7: 1, 8: 5, 9: 2, 10: 6, 11: 13, 12: 17, 13: 7, 14: 14, 15: 25, 16: 15, 17: 19, 18: 32, 19: 30, 21: 37, 22: 41, 23: 27, 24: 33, 25: 45, 26: 31, 27: 23, 28: 38, 29: 42, 30: 34, 31: 46, 32: 39, 33: 43, 34: 35, 35: 47},
    {8: 9, 10: 10, 12: 3, 13: 11, 14: 18, 15: 29, 16: 21, 17: 26, 18: 44, 19: 22},
)
LAST = {14: 0, 15: 1, 16: 2, 20: 3, 22: 4, 28: 6, 30: 7, 31: 5, 35: 9, 36: 10, 37: 8, 38: 11}
ROUTE = {35: 0, 36: 1, 38: 2}
PLACES = 15
STEPS = 39
SCORE = HD**-0.5 * 1.4426950408889634
MESH = pl.DeviceIdType.MESH


def places():
    s = lax.axis_index("seq")
    x, z, core = s // 4, (s // 2) % 2, s % 2

    def at(step, flip_z, flip_core):
        return ((x + step) % 4) * 4 + ((z + flip_z) % 2) * 2 + (core + flip_core) % 2

    return s, z, core, at


def slot(ref_k, ref_v, delta):
    g, r = (delta - 1) // GROUP, (delta - 1) % GROUP
    start = pl.multiple_of(r * ROWS, ROWS)
    return (
        ref_k.at[g, pl.ds(start, ROWS), pl.ds(0, HD)],
        ref_v.at[g, pl.ds(0, HD), pl.ds(start, ROWS)],
    )


def doc_of(ends, positions):
    doc = jnp.where(positions < 0, -1, 0)
    for end in ends:
        doc = doc + jnp.where(positions >= end, 1, 0)
    return doc


def pick(index, table):
    found = -1
    for key, value in table.items():
        found = jnp.where(index == key, value, found)
    return found


def one_of(chunk, units):
    found = chunk == units[0][0]
    for unit in units[1:]:
        found = found | (chunk == unit[0])
    return found


def attend_kernel(
    q_ref, k_ref, v_ref, len_ref, owner_ref, w_hbm, o_ref,
    qx, k_own, v_own, kx, vx, acc, top, fac, diff, s0, s1, p0, p1, att, w, parts,
    ring0, ring1, ring2,
    got0, got1, got2,
    rows0, rows1, rows2,
    parcels0, parcels1, parcels2,
    in0, in1, in2,
    out_from, in_from,
    send, recv, w_sem, ring_send, ring_recv, z_send, z_recv, parcel_send, parcel_recv,
):
    ring, got_z, rows, parcels, parcels_in = (
        (ring0, ring1, ring2),
        (got0, got1, got2),
        (rows0, rows1, rows2),
        (parcels0, parcels1, parcels2),
        (in0, in1, in2),
    )
    s, z, core, at = places()
    t = lax.axis_index("tp")
    z_lo, y = t // 4, t % 4
    sibling, next_x, prev_x, far_x, other_z = (
        at(0, 0, 1),
        at(1, 0, 0),
        at(3, 0, 0),
        at(2, 0, 0),
        at(0, 1, 0),
    )
    ahead, behind, partner = z_lo * 4 + (y + 1) % 4, z_lo * 4 + (y + 3) % 4, (1 - z_lo) * 4 + y
    load_w = pltpu.make_async_copy(w_hbm, w, w_sem)
    load_w.start()
    barrier = pltpu.get_barrier_semaphore()
    for k in range(1, SEQ):
        pl.semaphore_signal(
            barrier, inc=1, device_id={"seq": (s + k) % SEQ}, device_id_type=MESH
        )
    for peer in (ahead, behind, partner):
        pl.semaphore_signal(barrier, inc=1, device_id={"tp": peer}, device_id_type=MESH)

    k_own[:, :HD] = k_ref[...]
    v_own[:HD] = v_ref[...].T
    pl.semaphore_wait(barrier, SEQ - 1 + 3)

    def copy_of(index, source, target, peer, part):
        if source is None:
            a = (k_own.at[:, pl.ds(0, HD)], v_own.at[pl.ds(0, HD), :])[part]
        else:
            a = slot(kx, vx, source)[part]
        return pltpu.make_async_remote_copy(
            src_ref=a,
            dst_ref=slot(kx, vx, target)[part],
            send_sem=send.at[index, part],
            recv_sem=recv.at[target, part],
            device_id={"seq": peer},
            device_id_type=MESH,
        )

    def copies(index, source, target, peer):
        return [copy_of(index, source, target, peer, part) for part in range(2)]

    def go(index, source, target, peer, part):
        copy_of(index, source, target, peer, part).start()

    def arrived(target, part):
        copy_of(0, None, target, sibling, part).wait_recv()

    def pass_block(name, part):
        if name == 4:
            @pl.when(z == 1)
            def _():
                go(2, 4, 2, other_z, part)

            @pl.when(z == 0)
            def _():
                go(3, 4, 6, other_z, part)

        if name == 8:
            @pl.when(z == 1)
            def _():
                go(3, 8, 6, other_z, part)

        if name < 8:
            @pl.when(core == 0)
            def _():
                go(4 + name // 2, name, name + 1, sibling, part)

        @pl.when(core == 1)
        def _():
            go(3 + name // 2, name, name - 1, sibling, part)

    for part in range(2):
        go(0, None, 4, next_x, part)

        @pl.when(z == 0)
        def _():
            go(2, None, 2, other_z, part)

        @pl.when(core == 0)
        def _():
            go(4, None, 1, sibling, part)

    for part in range(2):
        go(1, None, 8, far_x, part)

    ends = []
    total = 0
    for d in range(4):
        total = total + len_ref[d]
        ends.append(total)
    lane = lax.broadcasted_iota(I32, (ROWS, HD), 1)
    row = lax.broadcasted_iota(I32, (ROWS, HD), 0)
    mine = jnp.where(doc_of(ends, row + s * ROWS) == lane, MASKED, 0.0).astype(BF16)
    for h in range(HEADS):
        for c in range(CHUNKS):
            queries = pl.ds(c * CHUNK, CHUNK)
            side = pl.ds(h % 2 * CHUNK, CHUNK)
            qx[c, h // 2, side, :HD] = q_ref[queries, h, :]
            qx[c, h // 2, side, HD:] = mine[c * CHUNK : (c + 1) * CHUNK]

    own_seen = doc_of(ends, row + s * ROWS) == lane
    k_own[:, HD:] = jnp.where(own_seen, 0.0, 1.0).astype(BF16)
    v_own[HD:] = jnp.ones((16, ROWS), BF16)

    diff[...] = lax.broadcasted_iota(I32, (ROWS, 2 * CHUNK), 0) - (
        lax.broadcasted_iota(I32, (ROWS, 2 * CHUNK), 1) % CHUNK
    )
    fac[...] = jnp.ones_like(fac)
    p1[...] = jnp.zeros_like(p1)

    scores, weights = (s0, s1), (p0, p1)

    both = (((1,), (1,)), ((), ()))

    def own_pass(i, _):
        @pl.when(i == 3)
        def _():
            arrived(4, 0)
            pass_block(4, 0)

        @pl.when(i == 5)
        def _():
            arrived(4, 1)
            pass_block(4, 1)

        c = i // 2
        pairs = (i % 2 * 2, i % 2 * 2 + 1)
        for par, p in enumerate(pairs):
            near = lax.dot_general(k_own[...], qx[c, p], both, preferred_element_type=F32)
            scores[par][:ROWS] = jnp.where(diff[...] <= c * CHUNK, near, MASKED)
        for par, p in enumerate(pairs):
            sc = scores[par][:ROWS]
            now = jnp.max(sc, axis=0, keepdims=True)
            top[c, p, :1, :] = now
            weight = jnp.exp2((sc - now) * SCORE).astype(BF16)
            acc[c, p] = jnp.dot(v_own[...], weight, preferred_element_type=F32)
        return 0

    lax.fori_loop(0, 2 * CHUNKS, own_pass, 0)

    def mark(delta, _):
        start = pl.multiple_of((delta - 1) % GROUP * ROWS, ROWS)
        seen = doc_of(ends, row + (s - delta) * ROWS) == lane
        kx[(delta - 1) // GROUP, pl.ds(start, ROWS), HD:] = jnp.where(seen, 0.0, 1.0).astype(BF16)
        return 0

    lax.fori_loop(1, BACK + 1, mark, 0)
    for g in range(2):
        vx[g, HD:, :] = jnp.ones((16, SPAN), BF16)
    for name in (2, 8):
        for part in range(2):
            arrived(name, part)
            pass_block(name, part)
    for part in range(2):
        arrived(1, part)
        arrived(3, part)

    def tile(n):
        b = n // PAIRS
        return b // 2, b % 2, n % PAIRS

    def score(n, out):
        c, g, p = tile(n)
        out[...] = lax.dot_general(kx[g], qx[c, p], both, preferred_element_type=F32)

    def weigh(n, par):
        c, g, p = tile(n)
        sc = scores[par][...]
        before = top[c, p, :1, :]
        now = jnp.maximum(before, jnp.max(sc, axis=0, keepdims=True))
        weights[par][...] = jnp.exp2((sc - now) * SCORE).astype(BF16)
        fac[par, :1, :] = jnp.exp2((before - now) * SCORE)
        top[c, p, :1, :] = now

    def mix(n, par):
        c, g, p = tile(n)
        acc[c, p] = acc[c, p] * fac[par, :1, :] + jnp.dot(
            vx[g], weights[par][...], preferred_element_type=F32
        )

    def ring_copy(j, c, k, way):
        return pltpu.make_async_remote_copy(
            src_ref=ring[j].at[c, k, way],
            dst_ref=ring[j].at[c, k + 1, way],
            send_sem=ring_send.at[j, c, k, way],
            recv_sem=ring_recv.at[j, c, k, way],
            device_id={"tp": (ahead, behind)[way]},
            device_id_type=MESH,
        )

    def z_copy(j, c):
        return pltpu.make_async_remote_copy(
            src_ref=ring[j].at[c, 3, 1 - z_lo],
            dst_ref=got_z[j].at[c],
            send_sem=z_send.at[j, c],
            recv_sem=z_recv.at[j, c],
            device_id={"tp": partner},
            device_id_type=MESH,
        )

    def share(c, k, way):
        owner = (y + 3 - k) % 4 if way == 0 else (y + 1 + k) % 4
        column = pl.multiple_of((way * 4 + owner) * WIDTH, HD)
        return jnp.dot(att[c], w[:, pl.ds(column, WIDTH)], preferred_element_type=F32)

    def finish(c):
        for h in range(HEADS):
            cols = pl.ds(h % 2 * CHUNK, CHUNK)
            part = acc[c, h // 2, :, cols]
            value = part[:HD] / part[HD : HD + 1]
            att[c, :, pl.ds(h * HD, HD)] = value.T.astype(BF16)
        for way in range(2):
            first = share(c, 0, way).astype(BF16)
            for j, (column, width) in enumerate(SLICES):
                ring[j][c, 0, way] = first[:, column : column + width]
            for j in range(PARTS):
                later = [u for u in LATE if u[1] == j]
                if later:
                    pl.when(jnp.logical_not(one_of(c, later)))(
                        lambda j=j, way=way: ring_copy(j, c, 0, way).start()
                    )
                else:
                    ring_copy(j, c, 0, way).start()

    def compute_shares(c, k):
        for way in range(2):
            parts[c, k - 1, way] = share(c, k, way)

    def pass_on(j, c, k):
        column, width = SLICES[j]

        @pl.when(k > 0)
        def _():
            for way in range(2):
                ring_copy(j, c, k - 1, way).wait_recv()
                mine = parts[c, k - 1, way, :, column : column + width]
                ring[j][c, k, way] = (ring[j][c, k, way].astype(F32) + mine).astype(BF16)

        @pl.when(k < 3)
        def _():
            for way in range(2):
                ring_copy(j, c, k, way).start()

        @pl.when(k == 3)
        def _():
            z_copy(j, c).start()

    def last(j, c):
        z_copy(j, c).wait_recv()
        total = ring[j][c, 3, z_lo].astype(F32) + got_z[j][c].astype(F32)
        rows[j][pl.ds(c * 4, 4)] = total.astype(BF16).reshape(4, PIECE, SLICES[j][1])

    def parcel(j, k):
        return pltpu.make_async_remote_copy(
            src_ref=parcels[j].at[k],
            dst_ref=parcels_in[j].at[k],
            send_sem=parcel_send.at[j, k],
            recv_sem=parcel_recv.at[j, k],
            device_id={"seq": (s + k) % SEQ},
            device_id_type=MESH,
        )

    def route(j):
        for k in range(1, SEQ):
            for r in range(2):
                parcels[j][k, r] = rows[j][out_from[(s + k) % SEQ * 2 + r]]
            parcel(j, k).start()
        for r in range(2):
            parcels_in[j][0, r] = rows[j][out_from[s * 2 + r]]

    score(0, s0)

    def step(i, _):
        @pl.when(i == 1)
        def _():
            for part in range(2):
                arrived(6, part)
                pass_block(6, part)
            for part in range(2):
                arrived(5, part)
                arrived(7, part)

        @pl.when(i == 5)
        def _():
            load_w.wait()

        @pl.when(i == PLACES)
        def _():
            own = [owner_ref[s * 16 + k] for k in range(16)]
            place = []
            for k in range(16):
                rank = 0
                for j in range(k):
                    rank = rank + jnp.where(own[j] == own[k], 1, 0)
                place.append(2 * own[k] + rank)
            for n in range(2 * SEQ):
                piece = 0
                for k in range(16):
                    piece = piece + jnp.where(place[k] == n, k, 0)
                out_from[n] = piece
            before = 0
            found = [0] * 16
            for source in range(SEQ):
                count = 0
                for k in range(16):
                    count = count + jnp.where(owner_ref[source * 16 + k] == s, 1, 0)
                far = (s - source + SEQ) % SEQ
                for j in range(16):
                    for r in range(2):
                        hit = (before + r == j) & (r < count)
                        found[j] = found[j] + jnp.where(hit, 2 * far + r, 0)
                before = before + count
            for j in range(16):
                in_from[j] = found[j]

        ready = pick(i, FINISH)

        @pl.when(ready >= 0)
        def _():
            finish(ready)

        shares = pick(i, SHARE)

        @pl.when(shares >= 0)
        def _():
            compute_shares(shares // 4, shares % 4)

        for table in PASS_ON:
            move = pick(i, table)
            for j in range(PARTS):

                @pl.when((move >= 0) & (move // 4 % PARTS == j))
                def _(j=j):
                    pass_on(j, move // (4 * PARTS), move % 4)

        done = pick(i, LAST)
        leave = pick(i, ROUTE)
        for j in range(PARTS):

            @pl.when((done >= 0) & (done % PARTS == j))
            def _(j=j):
                last(j, done // PARTS)

            @pl.when(leave == j)
            def _(j=j):
                route(j)

        @pl.when(i < TILES // 2)
        def _():
            score(2 * i + 1, s1)
            weigh(2 * i, 0)
            mix(jnp.maximum(2 * i - 1, 0), 1)
            score(jnp.minimum(2 * i + 2, TILES - 1), s0)
            weigh(2 * i + 1, 1)
            mix(2 * i, 0)

        @pl.when(i == TILES // 2)
        def _():
            mix(TILES - 1, 1)

        return 0

    lax.fori_loop(0, STEPS, step, 0)

    for j, (column, width) in enumerate(SLICES):
        for k in range(1, SEQ):
            parcel(j, k).wait_recv()
        for k in range(16):
            n = in_from[k]
            o_ref[pl.ds(k * PIECE, PIECE), column : column + width] = parcels_in[j][n // 2, n % 2]
    for j in range(PARTS):
        for k in range(1, SEQ):
            parcel(j, k).wait_send()

    for index in range(4):
        for copy in copies(index, 1, 1, sibling):
            copy.wait_send()
    for i in range(4):
        for copy in copies(4 + i, 1, 1, sibling):
            copy.wait_send()
    for j in range(PARTS):
        for c in range(CHUNKS):
            for k in range(3):
                for way in range(2):
                    ring_copy(j, c, k, way).wait_send()
            z_copy(j, c).wait_send()


def attention(queries, key_rows, value_rows, doc_lengths, piece_owner, out_weight):
    vmem = pl.BlockSpec(memory_space=pltpu.VMEM)
    return pl.pallas_call(
        attend_kernel,
        out_shape=jax.ShapeDtypeStruct((ROWS, WIDTH), BF16),
        in_specs=[
            vmem,
            vmem,
            vmem,
            pl.BlockSpec(memory_space=pltpu.SMEM),
            pl.BlockSpec(memory_space=pltpu.SMEM),
            pl.BlockSpec(memory_space=pl.ANY),
        ],
        out_specs=vmem,
        scratch_shapes=[
            pltpu.VMEM((CHUNKS, PAIRS, 2 * CHUNK, 2 * HD), BF16),
            pltpu.VMEM((ROWS, 2 * HD), BF16),
            pltpu.VMEM((HD + 16, ROWS), BF16),
            pltpu.VMEM((2, SPAN, 2 * HD), BF16),
            pltpu.VMEM((2, HD + 16, SPAN), BF16),
            pltpu.VMEM((CHUNKS, PAIRS, HD + 16, 2 * CHUNK), F32),
            pltpu.VMEM((CHUNKS, PAIRS, 8, 2 * CHUNK), F32),
            pltpu.VMEM((2, 8, 2 * CHUNK), F32),
            pltpu.VMEM((ROWS, 2 * CHUNK), I32),
            pltpu.VMEM((SPAN, 2 * CHUNK), F32),
            pltpu.VMEM((SPAN, 2 * CHUNK), F32),
            pltpu.VMEM((SPAN, 2 * CHUNK), BF16),
            pltpu.VMEM((SPAN, 2 * CHUNK), BF16),
            pltpu.VMEM((CHUNKS, CHUNK, HEADS * HD), BF16),
            pltpu.VMEM((HEADS * HD, 8 * WIDTH), BF16),
            pltpu.VMEM((CHUNKS, 3, 2, CHUNK, WIDTH), F32),
            *(pltpu.VMEM((CHUNKS, 4, 2, CHUNK, width), BF16) for _, width in SLICES),
            *(pltpu.VMEM((CHUNKS, CHUNK, width), BF16) for _, width in SLICES),
            *(pltpu.VMEM((16, PIECE, width), BF16) for _, width in SLICES),
            *(pltpu.VMEM((SEQ, 2, PIECE, width), BF16) for _, width in SLICES),
            *(pltpu.VMEM((SEQ, 2, PIECE, width), BF16) for _, width in SLICES),
            pltpu.SMEM((2 * SEQ,), I32),
            pltpu.SMEM((16,), I32),
            pltpu.SemaphoreType.DMA((8, 2)),
            pltpu.SemaphoreType.DMA((BACK + 1, 2)),
            pltpu.SemaphoreType.DMA,
            pltpu.SemaphoreType.DMA((PARTS, CHUNKS, 3, 2)),
            pltpu.SemaphoreType.DMA((PARTS, CHUNKS, 3, 2)),
            pltpu.SemaphoreType.DMA((PARTS, CHUNKS)),
            pltpu.SemaphoreType.DMA((PARTS, CHUNKS)),
            pltpu.SemaphoreType.DMA((PARTS, SEQ)),
            pltpu.SemaphoreType.DMA((PARTS, SEQ)),
        ],
        compiler_params=pltpu.CompilerParams(
            collective_id=0, has_side_effects=True, vmem_limit_bytes=56 << 20
        ),
    )(queries, key_rows, value_rows, doc_lengths, piece_owner, out_weight)


def on_device(queries, key_heads, value_heads, out_weight, doc_lengths, piece_owner):
    return attention(
        queries,
        key_heads.reshape(ROWS, HD),
        value_heads.reshape(ROWS, HD),
        doc_lengths,
        piece_owner,
        out_weight,
    )


def solution(mesh):
    placed = (
        P("seq", "tp", None),
        P("seq", "tp", None),
        P("seq", "tp", None),
        P("tp", None),
        P(),
        P(),
    )
    return jax.shard_map(
        on_device, mesh=mesh, in_specs=placed, out_specs=P("seq", "tp"), check_vma=False
    )
```

```python
import functools

import jax
import jax.numpy as jnp
from jax import lax
from jax.experimental import pallas as pl
from jax.experimental.pallas import tpu as pltpu
from jax.sharding import PartitionSpec as P

MASKED = -1e30
BF16, F32, I32 = jnp.bfloat16, jnp.float32, jnp.int32
ROWS = 512
HEADS = 8
HD = 128
WIDTH = 640
CHUNK = 128
CHUNKS = ROWS // CHUNK
PAIRS = HEADS // 2
GROUP = 4
SPAN = GROUP * ROWS
BACK = 8
PIECE = 32
SEQ = 16
TILES = 2 * CHUNKS * PAIRS
SLICES = ((0, 256), (256, 256), (512, 128))
PARTS = len(SLICES)
LATE = ((1, 2), (2, 2), (3, 2))
FINISH = {5: 0, 9: 1, 13: 2, 17: 3}
SHARE = {6: 1, 7: 2, 8: 3, 10: 5, 11: 6, 12: 7, 14: 9, 15: 10, 16: 11, 18: 13, 19: 14, 20: 15}
PASS_ON = (
    {7: 1, 8: 5, 9: 2, 10: 6, 11: 13, 12: 3, 13: 7, 14: 14, 15: 25, 16: 15, 17: 19, 18: 32, 19: 30, 21: 37, 22: 41, 23: 27, 24: 33, 25: 45, 26: 31, 27: 38, 28: 42, 29: 34, 30: 46, 31: 39, 32: 43, 33: 35, 34: 47},
    {8: 9, 9: 20, 10: 10, 11: 17, 12: 21, 13: 11, 14: 18, 15: 29, 16: 22, 17: 26, 18: 44, 19: 23},
)
LAST = {14: 0, 15: 1, 16: 2, 20: 3, 22: 4, 23: 5, 27: 6, 30: 7, 34: 9, 35: 10, 36: 8, 37: 11}
ROUTE = {34: 0, 35: 1, 37: 2}
PLACES = 15
STEPS = 38
SCORE = HD**-0.5 * 1.4426950408889634
MESH = pl.DeviceIdType.MESH


def places():
    s = lax.axis_index("seq")
    x, z, core = s // 4, (s // 2) % 2, s % 2

    def at(step, flip_z, flip_core):
        return ((x + step) % 4) * 4 + ((z + flip_z) % 2) * 2 + (core + flip_core) % 2

    return s, z, core, at


def slot(ref_k, ref_v, delta):
    g, r = (delta - 1) // GROUP, (delta - 1) % GROUP
    start = pl.multiple_of(r * ROWS, ROWS)
    return (
        ref_k.at[g, pl.ds(start, ROWS), pl.ds(0, HD)],
        ref_v.at[g, pl.ds(0, HD), pl.ds(start, ROWS)],
    )


def doc_of(ends, positions):
    doc = jnp.where(positions < 0, -1, 0)
    for end in ends:
        doc = doc + jnp.where(positions >= end, 1, 0)
    return doc


def pick(index, table):
    found = -1
    for key, value in table.items():
        found = jnp.where(index == key, value, found)
    return found


def one_of(chunk, units):
    found = chunk == units[0][0]
    for unit in units[1:]:
        found = found | (chunk == unit[0])
    return found


def attend_kernel(
    q_ref, k_ref, v_ref, len_ref, owner_ref, w_hbm, o_ref,
    qx, k_own, v_own, kx, vx, acc, top, fac, diff, s0, s1, p0, p1, att, w, parts,
    ring0, ring1, ring2,
    got0, got1, got2,
    rows0, rows1, rows2,
    parcels0, parcels1, parcels2,
    in0, in1, in2,
    out_from, in_from,
    send, recv, w_sem, ring_send, ring_recv, z_send, z_recv, parcel_send, parcel_recv,
):
    ring, got_z, rows, parcels, parcels_in = (
        (ring0, ring1, ring2),
        (got0, got1, got2),
        (rows0, rows1, rows2),
        (parcels0, parcels1, parcels2),
        (in0, in1, in2),
    )
    s, z, core, at = places()
    t = lax.axis_index("tp")
    z_lo, y = t // 4, t % 4
    sibling, next_x, prev_x, far_x, other_z = (
        at(0, 0, 1),
        at(1, 0, 0),
        at(3, 0, 0),
        at(2, 0, 0),
        at(0, 1, 0),
    )
    ahead, behind, partner = z_lo * 4 + (y + 1) % 4, z_lo * 4 + (y + 3) % 4, (1 - z_lo) * 4 + y
    load_w = pltpu.make_async_copy(w_hbm, w, w_sem)
    load_w.start()
    barrier = pltpu.get_barrier_semaphore()
    for k in range(1, SEQ):
        pl.semaphore_signal(
            barrier, inc=1, device_id={"seq": (s + k) % SEQ}, device_id_type=MESH
        )
    for peer in (ahead, behind, partner):
        pl.semaphore_signal(barrier, inc=1, device_id={"tp": peer}, device_id_type=MESH)

    k_own[:, :HD] = k_ref[...]
    v_own[:HD] = v_ref[...].T
    pl.semaphore_wait(barrier, SEQ - 1 + 3)

    def copy_of(index, source, target, peer, part):
        if source is None:
            a = (k_own.at[:, pl.ds(0, HD)], v_own.at[pl.ds(0, HD), :])[part]
        else:
            a = slot(kx, vx, source)[part]
        return pltpu.make_async_remote_copy(
            src_ref=a,
            dst_ref=slot(kx, vx, target)[part],
            send_sem=send.at[index, part],
            recv_sem=recv.at[target, part],
            device_id={"seq": peer},
            device_id_type=MESH,
        )

    def copies(index, source, target, peer):
        return [copy_of(index, source, target, peer, part) for part in range(2)]

    def go(index, source, target, peer, part):
        copy_of(index, source, target, peer, part).start()

    def arrived(target, part):
        copy_of(0, None, target, sibling, part).wait_recv()

    def pass_block(name, part):
        if name == 4:
            @pl.when(z == 1)
            def _():
                go(2, 4, 2, other_z, part)

            @pl.when(z == 0)
            def _():
                go(3, 4, 6, other_z, part)

        if name == 8:
            @pl.when(z == 1)
            def _():
                go(3, 8, 6, other_z, part)

        if name < 8:
            @pl.when(core == 0)
            def _():
                go(4 + name // 2, name, name + 1, sibling, part)

        @pl.when(core == 1)
        def _():
            go(3 + name // 2, name, name - 1, sibling, part)

    for part in range(2):
        go(0, None, 4, next_x, part)

        @pl.when(z == 0)
        def _():
            go(2, None, 2, other_z, part)

        @pl.when(core == 0)
        def _():
            go(4, None, 1, sibling, part)

    for part in range(2):
        go(1, None, 8, far_x, part)

    ends = []
    total = 0
    for d in range(4):
        total = total + len_ref[d]
        ends.append(total)
    lane = lax.broadcasted_iota(I32, (ROWS, HD), 1)
    row = lax.broadcasted_iota(I32, (ROWS, HD), 0)
    mine = jnp.where(doc_of(ends, row + s * ROWS) == lane, MASKED, 0.0).astype(BF16)
    for h in range(HEADS):
        for c in range(CHUNKS):
            queries = pl.ds(c * CHUNK, CHUNK)
            side = pl.ds(h % 2 * CHUNK, CHUNK)
            qx[c, h // 2, side, :HD] = q_ref[queries, h, :]
            qx[c, h // 2, side, HD:] = mine[c * CHUNK : (c + 1) * CHUNK]

    own_seen = doc_of(ends, row + s * ROWS) == lane
    k_own[:, HD:] = jnp.where(own_seen, 0.0, 1.0).astype(BF16)
    v_own[HD:] = jnp.ones((16, ROWS), BF16)

    diff[...] = lax.broadcasted_iota(I32, (ROWS, 2 * CHUNK), 0) - (
        lax.broadcasted_iota(I32, (ROWS, 2 * CHUNK), 1) % CHUNK
    )
    fac[...] = jnp.ones_like(fac)
    p1[...] = jnp.zeros_like(p1)

    scores, weights = (s0, s1), (p0, p1)

    both = (((1,), (1,)), ((), ()))

    def own_pass(i, _):
        @pl.when(i == 3)
        def _():
            arrived(4, 0)
            pass_block(4, 0)

        @pl.when(i == 5)
        def _():
            arrived(4, 1)
            pass_block(4, 1)

        c = i // 2
        pairs = (i % 2 * 2, i % 2 * 2 + 1)
        for par, p in enumerate(pairs):
            near = lax.dot_general(k_own[...], qx[c, p], both, preferred_element_type=F32)
            scores[par][:ROWS] = jnp.where(diff[...] <= c * CHUNK, near, MASKED)
        for par, p in enumerate(pairs):
            sc = scores[par][:ROWS]
            now = jnp.max(sc, axis=0, keepdims=True)
            top[c, p, :1, :] = now
            weight = jnp.exp2((sc - now) * SCORE).astype(BF16)
            acc[c, p] = jnp.dot(v_own[...], weight, preferred_element_type=F32)
        return 0

    lax.fori_loop(0, 2 * CHUNKS, own_pass, 0)

    def mark(delta, _):
        start = pl.multiple_of((delta - 1) % GROUP * ROWS, ROWS)
        seen = doc_of(ends, row + (s - delta) * ROWS) == lane
        kx[(delta - 1) // GROUP, pl.ds(start, ROWS), HD:] = jnp.where(seen, 0.0, 1.0).astype(BF16)
        return 0

    lax.fori_loop(1, BACK + 1, mark, 0)
    for g in range(2):
        vx[g, HD:, :] = jnp.ones((16, SPAN), BF16)
    for name in (2, 8):
        for part in range(2):
            arrived(name, part)
            pass_block(name, part)
    for part in range(2):
        arrived(1, part)
        arrived(3, part)

    def tile(n):
        b = n // PAIRS
        return b // 2, b % 2, n % PAIRS

    def score(n, out):
        c, g, p = tile(n)
        out[...] = lax.dot_general(kx[g], qx[c, p], both, preferred_element_type=F32)

    def weigh(n, par):
        c, g, p = tile(n)
        sc = scores[par][...]
        before = top[c, p, :1, :]
        now = jnp.maximum(before, jnp.max(sc, axis=0, keepdims=True))
        weights[par][...] = jnp.exp2((sc - now) * SCORE).astype(BF16)
        fac[par, :1, :] = jnp.exp2((before - now) * SCORE)
        top[c, p, :1, :] = now

    def mix(n, par):
        c, g, p = tile(n)
        acc[c, p] = acc[c, p] * fac[par, :1, :] + jnp.dot(
            vx[g], weights[par][...], preferred_element_type=F32
        )

    def ring_copy(j, c, k, way):
        return pltpu.make_async_remote_copy(
            src_ref=ring[j].at[c, k, way],
            dst_ref=ring[j].at[c, k + 1, way],
            send_sem=ring_send.at[j, c, k, way],
            recv_sem=ring_recv.at[j, c, k, way],
            device_id={"tp": (ahead, behind)[way]},
            device_id_type=MESH,
        )

    def z_copy(j, c):
        return pltpu.make_async_remote_copy(
            src_ref=ring[j].at[c, 3, 1 - z_lo],
            dst_ref=got_z[j].at[c],
            send_sem=z_send.at[j, c],
            recv_sem=z_recv.at[j, c],
            device_id={"tp": partner},
            device_id_type=MESH,
        )

    def share(c, k, way):
        owner = (y + 3 - k) % 4 if way == 0 else (y + 1 + k) % 4
        column = pl.multiple_of((way * 4 + owner) * WIDTH, HD)
        return jnp.dot(att[c], w[:, pl.ds(column, WIDTH)], preferred_element_type=F32)

    def finish(c):
        for h in range(HEADS):
            cols = pl.ds(h % 2 * CHUNK, CHUNK)
            part = acc[c, h // 2, :, cols]
            value = part[:HD] / part[HD : HD + 1]
            att[c, :, pl.ds(h * HD, HD)] = value.T.astype(BF16)
        for way in range(2):
            first = share(c, 0, way).astype(BF16)
            for j, (column, width) in enumerate(SLICES):
                ring[j][c, 0, way] = first[:, column : column + width]
            for j in range(PARTS):
                later = [u for u in LATE if u[1] == j]
                if later:
                    pl.when(jnp.logical_not(one_of(c, later)))(
                        lambda j=j, way=way: ring_copy(j, c, 0, way).start()
                    )
                else:
                    ring_copy(j, c, 0, way).start()

    def compute_shares(c, k):
        for way in range(2):
            parts[c, k - 1, way] = share(c, k, way)

    def pass_on(j, c, k):
        column, width = SLICES[j]

        @pl.when(k > 0)
        def _():
            for way in range(2):
                ring_copy(j, c, k - 1, way).wait_recv()
                mine = parts[c, k - 1, way, :, column : column + width]
                ring[j][c, k, way] = (ring[j][c, k, way].astype(F32) + mine).astype(BF16)

        @pl.when(k < 3)
        def _():
            for way in range(2):
                ring_copy(j, c, k, way).start()

        @pl.when(k == 3)
        def _():
            z_copy(j, c).start()

    def last(j, c):
        z_copy(j, c).wait_recv()
        total = ring[j][c, 3, z_lo].astype(F32) + got_z[j][c].astype(F32)
        rows[j][pl.ds(c * 4, 4)] = total.astype(BF16).reshape(4, PIECE, SLICES[j][1])

    def parcel(j, k):
        return pltpu.make_async_remote_copy(
            src_ref=parcels[j].at[k],
            dst_ref=parcels_in[j].at[k],
            send_sem=parcel_send.at[j, k],
            recv_sem=parcel_recv.at[j, k],
            device_id={"seq": (s + k) % SEQ},
            device_id_type=MESH,
        )

    def route(j):
        for k in range(1, SEQ):
            for r in range(2):
                parcels[j][k, r] = rows[j][out_from[(s + k) % SEQ * 2 + r]]
            parcel(j, k).start()
        for r in range(2):
            parcels_in[j][0, r] = rows[j][out_from[s * 2 + r]]

    score(0, s0)

    def step(i, _):
        @pl.when(i == 1)
        def _():
            for part in range(2):
                arrived(6, part)
                pass_block(6, part)
            for part in range(2):
                arrived(5, part)
                arrived(7, part)

        @pl.when(i == 5)
        def _():
            load_w.wait()

        @pl.when(i == PLACES)
        def _():
            own = [owner_ref[s * 16 + k] for k in range(16)]
            place = []
            for k in range(16):
                rank = 0
                for j in range(k):
                    rank = rank + jnp.where(own[j] == own[k], 1, 0)
                place.append(2 * own[k] + rank)
            for n in range(2 * SEQ):
                piece = 0
                for k in range(16):
                    piece = piece + jnp.where(place[k] == n, k, 0)
                out_from[n] = piece
            before = 0
            found = [0] * 16
            for source in range(SEQ):
                count = 0
                for k in range(16):
                    count = count + jnp.where(owner_ref[source * 16 + k] == s, 1, 0)
                far = (s - source + SEQ) % SEQ
                for j in range(16):
                    for r in range(2):
                        hit = (before + r == j) & (r < count)
                        found[j] = found[j] + jnp.where(hit, 2 * far + r, 0)
                before = before + count
            for j in range(16):
                in_from[j] = found[j]

        ready = pick(i, FINISH)

        @pl.when(ready >= 0)
        def _():
            finish(ready)

        shares = pick(i, SHARE)

        @pl.when(shares >= 0)
        def _():
            compute_shares(shares // 4, shares % 4)

        for table in PASS_ON:
            move = pick(i, table)
            for j in range(PARTS):

                @pl.when((move >= 0) & (move // 4 % PARTS == j))
                def _(j=j):
                    pass_on(j, move // (4 * PARTS), move % 4)

        done = pick(i, LAST)
        leave = pick(i, ROUTE)
        for j in range(PARTS):

            @pl.when((done >= 0) & (done % PARTS == j))
            def _(j=j):
                last(j, done // PARTS)

            @pl.when(leave == j)
            def _(j=j):
                route(j)

        @pl.when(i < TILES // 2)
        def _():
            score(2 * i + 1, s1)
            weigh(2 * i, 0)
            mix(jnp.maximum(2 * i - 1, 0), 1)
            score(jnp.minimum(2 * i + 2, TILES - 1), s0)
            weigh(2 * i + 1, 1)
            mix(2 * i, 0)

        @pl.when(i == TILES // 2)
        def _():
            mix(TILES - 1, 1)

        return 0

    lax.fori_loop(0, STEPS, step, 0)

    for j, (column, width) in enumerate(SLICES):
        for k in range(1, SEQ):
            parcel(j, k).wait_recv()
        for k in range(16):
            n = in_from[k]
            o_ref[pl.ds(k * PIECE, PIECE), column : column + width] = parcels_in[j][n // 2, n % 2]
    for j in range(PARTS):
        for k in range(1, SEQ):
            parcel(j, k).wait_send()

    for index in range(4):
        for copy in copies(index, 1, 1, sibling):
            copy.wait_send()
    for i in range(4):
        for copy in copies(4 + i, 1, 1, sibling):
            copy.wait_send()
    for j in range(PARTS):
        for c in range(CHUNKS):
            for k in range(3):
                for way in range(2):
                    ring_copy(j, c, k, way).wait_send()
            z_copy(j, c).wait_send()


def attention(queries, key_rows, value_rows, doc_lengths, piece_owner, out_weight):
    vmem = pl.BlockSpec(memory_space=pltpu.VMEM)
    return pl.pallas_call(
        attend_kernel,
        out_shape=jax.ShapeDtypeStruct((ROWS, WIDTH), BF16),
        in_specs=[
            vmem,
            vmem,
            vmem,
            pl.BlockSpec(memory_space=pltpu.SMEM),
            pl.BlockSpec(memory_space=pltpu.SMEM),
            pl.BlockSpec(memory_space=pl.ANY),
        ],
        out_specs=vmem,
        scratch_shapes=[
            pltpu.VMEM((CHUNKS, PAIRS, 2 * CHUNK, 2 * HD), BF16),
            pltpu.VMEM((ROWS, 2 * HD), BF16),
            pltpu.VMEM((HD + 16, ROWS), BF16),
            pltpu.VMEM((2, SPAN, 2 * HD), BF16),
            pltpu.VMEM((2, HD + 16, SPAN), BF16),
            pltpu.VMEM((CHUNKS, PAIRS, HD + 16, 2 * CHUNK), F32),
            pltpu.VMEM((CHUNKS, PAIRS, 8, 2 * CHUNK), F32),
            pltpu.VMEM((2, 8, 2 * CHUNK), F32),
            pltpu.VMEM((ROWS, 2 * CHUNK), I32),
            pltpu.VMEM((SPAN, 2 * CHUNK), F32),
            pltpu.VMEM((SPAN, 2 * CHUNK), F32),
            pltpu.VMEM((SPAN, 2 * CHUNK), BF16),
            pltpu.VMEM((SPAN, 2 * CHUNK), BF16),
            pltpu.VMEM((CHUNKS, CHUNK, HEADS * HD), BF16),
            pltpu.VMEM((HEADS * HD, 8 * WIDTH), BF16),
            pltpu.VMEM((CHUNKS, 3, 2, CHUNK, WIDTH), F32),
            *(pltpu.VMEM((CHUNKS, 4, 2, CHUNK, width), BF16) for _, width in SLICES),
            *(pltpu.VMEM((CHUNKS, CHUNK, width), BF16) for _, width in SLICES),
            *(pltpu.VMEM((16, PIECE, width), BF16) for _, width in SLICES),
            *(pltpu.VMEM((SEQ, 2, PIECE, width), BF16) for _, width in SLICES),
            *(pltpu.VMEM((SEQ, 2, PIECE, width), BF16) for _, width in SLICES),
            pltpu.SMEM((2 * SEQ,), I32),
            pltpu.SMEM((16,), I32),
            pltpu.SemaphoreType.DMA((8, 2)),
            pltpu.SemaphoreType.DMA((BACK + 1, 2)),
            pltpu.SemaphoreType.DMA,
            pltpu.SemaphoreType.DMA((PARTS, CHUNKS, 3, 2)),
            pltpu.SemaphoreType.DMA((PARTS, CHUNKS, 3, 2)),
            pltpu.SemaphoreType.DMA((PARTS, CHUNKS)),
            pltpu.SemaphoreType.DMA((PARTS, CHUNKS)),
            pltpu.SemaphoreType.DMA((PARTS, SEQ)),
            pltpu.SemaphoreType.DMA((PARTS, SEQ)),
        ],
        compiler_params=pltpu.CompilerParams(
            collective_id=0, has_side_effects=True, vmem_limit_bytes=56 << 20
        ),
    )(queries, key_rows, value_rows, doc_lengths, piece_owner, out_weight)


def on_device(queries, key_heads, value_heads, out_weight, doc_lengths, piece_owner):
    return attention(
        queries,
        key_heads.reshape(ROWS, HD),
        value_heads.reshape(ROWS, HD),
        doc_lengths,
        piece_owner,
        out_weight,
    )


def solution(mesh):
    placed = (
        P("seq", "tp", None),
        P("seq", "tp", None),
        P("seq", "tp", None),
        P("tp", None),
        P(),
        P(),
    )
    return jax.shard_map(
        on_device, mesh=mesh, in_specs=placed, out_specs=P("seq", "tp"), check_vma=False
    )
```

```python
import functools

import jax
import jax.numpy as jnp
from jax import lax
from jax.experimental import pallas as pl
from jax.experimental.pallas import tpu as pltpu
from jax.sharding import PartitionSpec as P

MASKED = -1e30
BF16, F32, I32 = jnp.bfloat16, jnp.float32, jnp.int32
ROWS = 512
HEADS = 8
HD = 128
WIDTH = 640
CHUNK = 128
CHUNKS = ROWS // CHUNK
PAIRS = HEADS // 2
GROUP = 4
SPAN = GROUP * ROWS
BACK = 8
PIECE = 32
SEQ = 16
TILES = 2 * CHUNKS * PAIRS
SLICES = ((0, 256), (256, 256), (512, 128))
PARTS = len(SLICES)
LATE = ((1, 2), (2, 2), (3, 2))
FINISH = {5: 0, 9: 1, 13: 2, 17: 3}
SHARE = {6: 1, 7: 2, 8: 3, 10: 5, 11: 6, 12: 7, 14: 9, 15: 10, 16: 11, 18: 13, 19: 14, 20: 15}
PASS_ON = (
    {7: 1, 8: 5, 9: 2, 10: 6, 11: 13, 12: 3, 13: 7, 14: 14, 15: 25, 16: 15, 17: 19, 18: 32, 19: 30, 21: 37, 22: 41, 23: 27, 24: 33, 25: 45, 26: 31, 27: 38, 28: 42, 29: 34, 30: 46, 31: 39, 32: 43, 33: 35, 34: 47},
    {8: 9, 9: 20, 10: 10, 11: 17, 12: 21, 13: 11, 14: 18, 15: 29, 16: 22, 17: 26, 18: 44, 19: 23},
)
LAST = {14: 0, 15: 1, 16: 2, 20: 3, 22: 4, 23: 5, 27: 6, 30: 7, 34: 9, 35: 10, 36: 8, 37: 11}
ROUTE = {34: 0, 35: 1, 37: 2}
PLACES = 15
STEPS = 38
SCORE = HD**-0.5 * 1.4426950408889634
MESH = pl.DeviceIdType.MESH


def places():
    s = lax.axis_index("seq")
    x, z, core = s // 4, (s // 2) % 2, s % 2

    def at(step, flip_z, flip_core):
        return ((x + step) % 4) * 4 + ((z + flip_z) % 2) * 2 + (core + flip_core) % 2

    return s, z, core, at


def slot(ref_k, ref_v, delta):
    g, r = (delta - 1) // GROUP, (delta - 1) % GROUP
    start = pl.multiple_of(r * ROWS, ROWS)
    return (
        ref_k.at[g, pl.ds(start, ROWS), pl.ds(0, HD)],
        ref_v.at[g, pl.ds(0, HD), pl.ds(start, ROWS)],
    )


def doc_of(ends, positions):
    doc = jnp.where(positions < 0, -1, 0)
    for end in ends:
        doc = doc + jnp.where(positions >= end, 1, 0)
    return doc


def pick(index, table):
    found = -1
    for key, value in table.items():
        found = jnp.where(index == key, value, found)
    return found


def one_of(chunk, units):
    found = chunk == units[0][0]
    for unit in units[1:]:
        found = found | (chunk == unit[0])
    return found


def attend_kernel(
    q_ref, k_ref, v_ref, len_ref, owner_ref, w_hbm, o_ref,
    qx, k_own, v_own, kx, vx, acc, top, fac, diff, s0, s1, p0, p1, att, w, parts,
    ring0, ring1, ring2,
    got0, got1, got2,
    rows0, rows1, rows2,
    parcels0, parcels1, parcels2,
    in0, in1, in2,
    out_from, in_from,
    send, recv, w_sem, ring_send, ring_recv, z_send, z_recv, parcel_send, parcel_recv,
):
    ring, got_z, rows, parcels, parcels_in = (
        (ring0, ring1, ring2),
        (got0, got1, got2),
        (rows0, rows1, rows2),
        (parcels0, parcels1, parcels2),
        (in0, in1, in2),
    )
    s, z, core, at = places()
    t = lax.axis_index("tp")
    z_lo, y = t // 4, t % 4
    sibling, next_x, prev_x, far_x, other_z = (
        at(0, 0, 1),
        at(1, 0, 0),
        at(3, 0, 0),
        at(2, 0, 0),
        at(0, 1, 0),
    )
    ahead, behind, partner = z_lo * 4 + (y + 1) % 4, z_lo * 4 + (y + 3) % 4, (1 - z_lo) * 4 + y
    load_w = pltpu.make_async_copy(w_hbm, w, w_sem)
    load_w.start()
    barrier = pltpu.get_barrier_semaphore()
    for k in range(1, SEQ):
        pl.semaphore_signal(
            barrier, inc=1, device_id={"seq": (s + k) % SEQ}, device_id_type=MESH
        )
    for peer in (ahead, behind, partner):
        pl.semaphore_signal(barrier, inc=1, device_id={"tp": peer}, device_id_type=MESH)

    k_own[:, :HD] = k_ref[...]
    v_own[:HD] = v_ref[...].T
    pl.semaphore_wait(barrier, SEQ - 1 + 3)

    def copy_of(index, source, target, peer, part):
        if source is None:
            a = (k_own.at[:, pl.ds(0, HD)], v_own.at[pl.ds(0, HD), :])[part]
        else:
            a = slot(kx, vx, source)[part]
        return pltpu.make_async_remote_copy(
            src_ref=a,
            dst_ref=slot(kx, vx, target)[part],
            send_sem=send.at[index, part],
            recv_sem=recv.at[target, part],
            device_id={"seq": peer},
            device_id_type=MESH,
        )

    def copies(index, source, target, peer):
        return [copy_of(index, source, target, peer, part) for part in range(2)]

    def go(index, source, target, peer, part):
        copy_of(index, source, target, peer, part).start()

    def arrived(target, part):
        copy_of(0, None, target, sibling, part).wait_recv()

    def pass_block(name, part):
        if name == 4:
            @pl.when(z == 1)
            def _():
                go(2, 4, 2, other_z, part)

            @pl.when(z == 0)
            def _():
                go(3, 4, 6, other_z, part)

        if name == 8:
            @pl.when(z == 1)
            def _():
                go(3, 8, 6, other_z, part)

        if name < 8:
            @pl.when(core == 0)
            def _():
                go(4 + name // 2, name, name + 1, sibling, part)

        @pl.when(core == 1)
        def _():
            go(3 + name // 2, name, name - 1, sibling, part)

    for part in range(2):
        go(0, None, 4, next_x, part)

        @pl.when(z == 0)
        def _():
            go(2, None, 2, other_z, part)

        @pl.when(core == 0)
        def _():
            go(4, None, 1, sibling, part)

    go(1, None, 8, far_x, 0)

    ends = []
    total = 0
    for d in range(4):
        total = total + len_ref[d]
        ends.append(total)
    lane = lax.broadcasted_iota(I32, (ROWS, HD), 1)
    row = lax.broadcasted_iota(I32, (ROWS, HD), 0)
    mine = jnp.where(doc_of(ends, row + s * ROWS) == lane, MASKED, 0.0).astype(BF16)
    for h in range(HEADS):
        for c in range(CHUNKS):
            queries = pl.ds(c * CHUNK, CHUNK)
            side = pl.ds(h % 2 * CHUNK, CHUNK)
            qx[c, h // 2, side, :HD] = q_ref[queries, h, :]
            qx[c, h // 2, side, HD:] = mine[c * CHUNK : (c + 1) * CHUNK]

    own_seen = doc_of(ends, row + s * ROWS) == lane
    k_own[:, HD:] = jnp.where(own_seen, 0.0, 1.0).astype(BF16)
    v_own[HD:] = jnp.ones((16, ROWS), BF16)

    diff[...] = lax.broadcasted_iota(I32, (ROWS, 2 * CHUNK), 0) - (
        lax.broadcasted_iota(I32, (ROWS, 2 * CHUNK), 1) % CHUNK
    )
    fac[...] = jnp.ones_like(fac)
    p1[...] = jnp.zeros_like(p1)

    scores, weights = (s0, s1), (p0, p1)

    both = (((1,), (1,)), ((), ()))

    def own_pass(i, _):
        @pl.when(i == 3)
        def _():
            arrived(4, 0)
            pass_block(4, 0)

        @pl.when(i == 5)
        def _():
            arrived(4, 1)
            pass_block(4, 1)
            go(1, None, 8, far_x, 1)

        c = i // 2
        pairs = (i % 2 * 2, i % 2 * 2 + 1)
        for par, p in enumerate(pairs):
            near = lax.dot_general(k_own[...], qx[c, p], both, preferred_element_type=F32)
            scores[par][:ROWS] = jnp.where(diff[...] <= c * CHUNK, near, MASKED)
        for par, p in enumerate(pairs):
            sc = scores[par][:ROWS]
            now = jnp.max(sc, axis=0, keepdims=True)
            top[c, p, :1, :] = now
            weight = jnp.exp2((sc - now) * SCORE).astype(BF16)
            acc[c, p] = jnp.dot(v_own[...], weight, preferred_element_type=F32)
        return 0

    lax.fori_loop(0, 2 * CHUNKS, own_pass, 0)

    def mark(delta, _):
        start = pl.multiple_of((delta - 1) % GROUP * ROWS, ROWS)
        seen = doc_of(ends, row + (s - delta) * ROWS) == lane
        kx[(delta - 1) // GROUP, pl.ds(start, ROWS), HD:] = jnp.where(seen, 0.0, 1.0).astype(BF16)
        return 0

    lax.fori_loop(1, BACK + 1, mark, 0)
    for g in range(2):
        vx[g, HD:, :] = jnp.ones((16, SPAN), BF16)
    for name in (2, 8):
        for part in range(2):
            arrived(name, part)
            pass_block(name, part)
    for part in range(2):
        arrived(1, part)
        arrived(3, part)

    def tile(n):
        b = n // PAIRS
        return b // 2, b % 2, n % PAIRS

    def score(n, out):
        c, g, p = tile(n)
        out[...] = lax.dot_general(kx[g], qx[c, p], both, preferred_element_type=F32)

    def weigh(n, par):
        c, g, p = tile(n)
        sc = scores[par][...]
        before = top[c, p, :1, :]
        now = jnp.maximum(before, jnp.max(sc, axis=0, keepdims=True))
        weights[par][...] = jnp.exp2((sc - now) * SCORE).astype(BF16)
        fac[par, :1, :] = jnp.exp2((before - now) * SCORE)
        top[c, p, :1, :] = now

    def mix(n, par):
        c, g, p = tile(n)
        acc[c, p] = acc[c, p] * fac[par, :1, :] + jnp.dot(
            vx[g], weights[par][...], preferred_element_type=F32
        )

    def ring_copy(j, c, k, way):
        return pltpu.make_async_remote_copy(
            src_ref=ring[j].at[c, k, way],
            dst_ref=ring[j].at[c, k + 1, way],
            send_sem=ring_send.at[j, c, k, way],
            recv_sem=ring_recv.at[j, c, k, way],
            device_id={"tp": (ahead, behind)[way]},
            device_id_type=MESH,
        )

    def z_copy(j, c):
        return pltpu.make_async_remote_copy(
            src_ref=ring[j].at[c, 3, 1 - z_lo],
            dst_ref=got_z[j].at[c],
            send_sem=z_send.at[j, c],
            recv_sem=z_recv.at[j, c],
            device_id={"tp": partner},
            device_id_type=MESH,
        )

    def share(c, k, way):
        owner = (y + 3 - k) % 4 if way == 0 else (y + 1 + k) % 4
        column = pl.multiple_of((way * 4 + owner) * WIDTH, HD)
        return jnp.dot(att[c], w[:, pl.ds(column, WIDTH)], preferred_element_type=F32)

    def finish(c):
        for h in range(HEADS):
            cols = pl.ds(h % 2 * CHUNK, CHUNK)
            part = acc[c, h // 2, :, cols]
            value = part[:HD] / part[HD : HD + 1]
            att[c, :, pl.ds(h * HD, HD)] = value.T.astype(BF16)
        for way in range(2):
            first = share(c, 0, way).astype(BF16)
            for j, (column, width) in enumerate(SLICES):
                ring[j][c, 0, way] = first[:, column : column + width]
            for j in range(PARTS):
                later = [u for u in LATE if u[1] == j]
                if later:
                    pl.when(jnp.logical_not(one_of(c, later)))(
                        lambda j=j, way=way: ring_copy(j, c, 0, way).start()
                    )
                else:
                    ring_copy(j, c, 0, way).start()

    def compute_shares(c, k):
        for way in range(2):
            parts[c, k - 1, way] = share(c, k, way)

    def pass_on(j, c, k):
        column, width = SLICES[j]

        @pl.when(k > 0)
        def _():
            for way in range(2):
                ring_copy(j, c, k - 1, way).wait_recv()
                mine = parts[c, k - 1, way, :, column : column + width]
                ring[j][c, k, way] = (ring[j][c, k, way].astype(F32) + mine).astype(BF16)

        @pl.when(k < 3)
        def _():
            for way in range(2):
                ring_copy(j, c, k, way).start()

        @pl.when(k == 3)
        def _():
            z_copy(j, c).start()

    def last(j, c):
        z_copy(j, c).wait_recv()
        total = ring[j][c, 3, z_lo].astype(F32) + got_z[j][c].astype(F32)
        rows[j][pl.ds(c * 4, 4)] = total.astype(BF16).reshape(4, PIECE, SLICES[j][1])

    def parcel(j, k):
        return pltpu.make_async_remote_copy(
            src_ref=parcels[j].at[k],
            dst_ref=parcels_in[j].at[k],
            send_sem=parcel_send.at[j, k],
            recv_sem=parcel_recv.at[j, k],
            device_id={"seq": (s + k) % SEQ},
            device_id_type=MESH,
        )

    def route(j):
        for k in range(1, SEQ):
            for r in range(2):
                parcels[j][k, r] = rows[j][out_from[(s + k) % SEQ * 2 + r]]
            parcel(j, k).start()
        for r in range(2):
            parcels_in[j][0, r] = rows[j][out_from[s * 2 + r]]

    score(0, s0)

    def step(i, _):
        @pl.when(i == 1)
        def _():
            for part in range(2):
                arrived(6, part)
                pass_block(6, part)
            for part in range(2):
                arrived(5, part)
                arrived(7, part)

        @pl.when(i == 5)
        def _():
            load_w.wait()

        @pl.when(i == PLACES)
        def _():
            own = [owner_ref[s * 16 + k] for k in range(16)]
            place = []
            for k in range(16):
                rank = 0
                for j in range(k):
                    rank = rank + jnp.where(own[j] == own[k], 1, 0)
                place.append(2 * own[k] + rank)
            for n in range(2 * SEQ):
                piece = 0
                for k in range(16):
                    piece = piece + jnp.where(place[k] == n, k, 0)
                out_from[n] = piece
            before = 0
            found = [0] * 16
            for source in range(SEQ):
                count = 0
                for k in range(16):
                    count = count + jnp.where(owner_ref[source * 16 + k] == s, 1, 0)
                far = (s - source + SEQ) % SEQ
                for j in range(16):
                    for r in range(2):
                        hit = (before + r == j) & (r < count)
                        found[j] = found[j] + jnp.where(hit, 2 * far + r, 0)
                before = before + count
            for j in range(16):
                in_from[j] = found[j]

        ready = pick(i, FINISH)

        @pl.when(ready >= 0)
        def _():
            finish(ready)

        shares = pick(i, SHARE)

        @pl.when(shares >= 0)
        def _():
            compute_shares(shares // 4, shares % 4)

        for table in PASS_ON:
            move = pick(i, table)
            for j in range(PARTS):

                @pl.when((move >= 0) & (move // 4 % PARTS == j))
                def _(j=j):
                    pass_on(j, move // (4 * PARTS), move % 4)

        done = pick(i, LAST)
        leave = pick(i, ROUTE)
        for j in range(PARTS):

            @pl.when((done >= 0) & (done % PARTS == j))
            def _(j=j):
                last(j, done // PARTS)

            @pl.when(leave == j)
            def _(j=j):
                route(j)

        @pl.when(i < TILES // 2)
        def _():
            score(2 * i + 1, s1)
            weigh(2 * i, 0)
            mix(jnp.maximum(2 * i - 1, 0), 1)
            score(jnp.minimum(2 * i + 2, TILES - 1), s0)
            weigh(2 * i + 1, 1)
            mix(2 * i, 0)

        @pl.when(i == TILES // 2)
        def _():
            mix(TILES - 1, 1)

        return 0

    lax.fori_loop(0, STEPS, step, 0)

    for j, (column, width) in enumerate(SLICES):
        for k in range(1, SEQ):
            parcel(j, k).wait_recv()
        for k in range(16):
            n = in_from[k]
            o_ref[pl.ds(k * PIECE, PIECE), column : column + width] = parcels_in[j][n // 2, n % 2]
    for j in range(PARTS):
        for k in range(1, SEQ):
            parcel(j, k).wait_send()

    for index in range(4):
        for copy in copies(index, 1, 1, sibling):
            copy.wait_send()
    for i in range(4):
        for copy in copies(4 + i, 1, 1, sibling):
            copy.wait_send()
    for j in range(PARTS):
        for c in range(CHUNKS):
            for k in range(3):
                for way in range(2):
                    ring_copy(j, c, k, way).wait_send()
            z_copy(j, c).wait_send()


def attention(queries, key_rows, value_rows, doc_lengths, piece_owner, out_weight):
    vmem = pl.BlockSpec(memory_space=pltpu.VMEM)
    return pl.pallas_call(
        attend_kernel,
        out_shape=jax.ShapeDtypeStruct((ROWS, WIDTH), BF16),
        in_specs=[
            vmem,
            vmem,
            vmem,
            pl.BlockSpec(memory_space=pltpu.SMEM),
            pl.BlockSpec(memory_space=pltpu.SMEM),
            pl.BlockSpec(memory_space=pl.ANY),
        ],
        out_specs=vmem,
        scratch_shapes=[
            pltpu.VMEM((CHUNKS, PAIRS, 2 * CHUNK, 2 * HD), BF16),
            pltpu.VMEM((ROWS, 2 * HD), BF16),
            pltpu.VMEM((HD + 16, ROWS), BF16),
            pltpu.VMEM((2, SPAN, 2 * HD), BF16),
            pltpu.VMEM((2, HD + 16, SPAN), BF16),
            pltpu.VMEM((CHUNKS, PAIRS, HD + 16, 2 * CHUNK), F32),
            pltpu.VMEM((CHUNKS, PAIRS, 8, 2 * CHUNK), F32),
            pltpu.VMEM((2, 8, 2 * CHUNK), F32),
            pltpu.VMEM((ROWS, 2 * CHUNK), I32),
            pltpu.VMEM((SPAN, 2 * CHUNK), F32),
            pltpu.VMEM((SPAN, 2 * CHUNK), F32),
            pltpu.VMEM((SPAN, 2 * CHUNK), BF16),
            pltpu.VMEM((SPAN, 2 * CHUNK), BF16),
            pltpu.VMEM((CHUNKS, CHUNK, HEADS * HD), BF16),
            pltpu.VMEM((HEADS * HD, 8 * WIDTH), BF16),
            pltpu.VMEM((CHUNKS, 3, 2, CHUNK, WIDTH), F32),
            *(pltpu.VMEM((CHUNKS, 4, 2, CHUNK, width), BF16) for _, width in SLICES),
            *(pltpu.VMEM((CHUNKS, CHUNK, width), BF16) for _, width in SLICES),
            *(pltpu.VMEM((16, PIECE, width), BF16) for _, width in SLICES),
            *(pltpu.VMEM((SEQ, 2, PIECE, width), BF16) for _, width in SLICES),
            *(pltpu.VMEM((SEQ, 2, PIECE, width), BF16) for _, width in SLICES),
            pltpu.SMEM((2 * SEQ,), I32),
            pltpu.SMEM((16,), I32),
            pltpu.SemaphoreType.DMA((8, 2)),
            pltpu.SemaphoreType.DMA((BACK + 1, 2)),
            pltpu.SemaphoreType.DMA,
            pltpu.SemaphoreType.DMA((PARTS, CHUNKS, 3, 2)),
            pltpu.SemaphoreType.DMA((PARTS, CHUNKS, 3, 2)),
            pltpu.SemaphoreType.DMA((PARTS, CHUNKS)),
            pltpu.SemaphoreType.DMA((PARTS, CHUNKS)),
            pltpu.SemaphoreType.DMA((PARTS, SEQ)),
            pltpu.SemaphoreType.DMA((PARTS, SEQ)),
        ],
        compiler_params=pltpu.CompilerParams(
            collective_id=0, has_side_effects=True, vmem_limit_bytes=56 << 20
        ),
    )(queries, key_rows, value_rows, doc_lengths, piece_owner, out_weight)


def on_device(queries, key_heads, value_heads, out_weight, doc_lengths, piece_owner):
    return attention(
        queries,
        key_heads.reshape(ROWS, HD),
        value_heads.reshape(ROWS, HD),
        doc_lengths,
        piece_owner,
        out_weight,
    )


def solution(mesh):
    placed = (
        P("seq", "tp", None),
        P("seq", "tp", None),
        P("seq", "tp", None),
        P("tp", None),
        P(),
        P(),
    )
    return jax.shard_map(
        on_device, mesh=mesh, in_specs=placed, out_specs=P("seq", "tp"), check_vma=False
    )
```
